32 devices in a mesh: parts: 16 (over z, y, x), mp: 2 (over core).
Axes of the slice: x: 2, y: 2, z: 4, core: 2. Of those that a mesh axis runs over, the one named last changes fastest.
Arguments:
- features: bfloat16 [4, 6144, 2048], P('mp', 'parts'), may hold values from -6 to 6
- weight: bfloat16 [2048, 2048], P('mp'), may hold values from -0.25 to 0.25
- bias: bfloat16 [2048], P('mp'), may hold values from -3 to 3
- local_adj: int32 [4, 6144, 384], P('mp', 'parts'), may hold values from 0 to 1, as said below
- send_index: int32 [4, 16, 16, 4], P('mp', 'parts'), may hold values from -1 to 383, as said below
- recv_target: int32 [4, 16, 16, 4], P('mp', 'parts'), may hold values from -1 to 383, as said below
- cotangent: bfloat16 [4, 6144, 2048], P('mp', 'parts'), may hold values from -6 to 6
Outputs:
- activations: bfloat16 [4, 6144, 2048], P('mp', 'parts')
- input_grad: bfloat16 [4, 6144, 2048], P('mp', 'parts')
- weight_grad: float32 [2048, 2048], P(('parts', 'mp'))
- bias_grad: float32 [2048], P(('parts', 'mp'))
The draws below stay inside these ranges and needn't reach their ends.
Inputs may be any that keep to these rules, and one draw needn't show every extreme that they name: `local_adj`: 0 or 1, zero on the diagonal of every part's block. `send_index`: -1 marks an unused slot; slot (p, q, h) is used exactly when slot (q, p, h) of recv_target is; used slots of a pair come first; no part sends to itself; some pairs use all 4 slots. `recv_target`: -1 marks an unused slot, used exactly as in send_index with the two part dimensions swapped.
All inputs are finite; a program needn't handle non-finite values.
Results may differ from the reference program's by a relative error of at most 0.006.
Values may be sent and summed in bfloat16 or wider, within the bound.
No kernel may reach another device: no remote copies, remote signals or barrier semaphores. Data moves between devices by JAX's collectives and lax.ppermute only.
A program may use at most 128 MiB of HBM per device.

```python
import jax
import jax.numpy as jnp
from jax import lax

D = 2048
PN = 384
HALO = 4
MICRO = 4
NODES = 6144
N_PARTS = 16


def halo_layout(key):
    key_heavy, key_fill, key_src, key_dst = jax.random.split(key, 4)
    ranks = jax.vmap(lambda sub: jax.random.permutation(sub, N_PARTS))(jax.random.split(key_heavy, MICRO))
    heavy = ranks < max(1, N_PARTS // 8)
    pair_heavy = heavy[:, :, None] | heavy[:, None, :]
    light = jax.random.randint(key_fill, (MICRO, N_PARTS, N_PARTS), 1, HALO // 2 + 1)
    count = jnp.where(pair_heavy, HALO, light)
    same_part = jnp.arange(N_PARTS)[:, None] == jnp.arange(N_PARTS)[None, :]
    count = jnp.where(same_part[None, :, :], 0, count)
    used = jnp.arange(HALO)[None, None, None, :] < count[:, :, :, None]
    shape = (MICRO, N_PARTS, N_PARTS, HALO)
    sender = jnp.where(used, jax.random.randint(key_src, shape, 0, PN), -1)
    target = jnp.where(used, jax.random.randint(key_dst, shape, 0, PN), -1)
    return (sender.astype(jnp.int32), jnp.transpose(target, (0, 2, 1, 3)).astype(jnp.int32))


def draw_send_index(key, part):
    sender, target = halo_layout(key)
    return sender


def draw_recv_target(key, part):
    sender, target = halo_layout(key)
    return target


def draw_local_adj(key, part):
    key = jax.random.fold_in(key, 7)
    key_level, key_edge = jax.random.split(key)
    tile = min(128, PN)
    tiles = PN // tile
    table = jnp.array([0, 1, 2, 4], jnp.int32)
    level = table[jax.random.randint(key_level, (MICRO, N_PARTS, tiles, tiles), 0, 4)]
    level = jnp.repeat(jnp.repeat(level, tile, axis=2), tile, axis=3)
    spread = jax.random.randint(key_edge, (MICRO, N_PARTS, PN, PN), 0, 2 * PN)
    edges = spread < 7 * level
    diagonal = jnp.arange(PN)[:, None] == jnp.arange(PN)[None, :]
    edges = edges & jnp.logical_not(diagonal)[None, None]
    return edges.astype(jnp.int32).reshape(MICRO, N_PARTS * PN, PN)


def block_levels(key, extent, cuts, low, largest):
    gain = 1.0
    for position, parts in cuts:
        heights = jax.random.uniform(jax.random.fold_in(jax.random.fold_in(key, 6), position), (parts,), jnp.float32, low / len(cuts), largest / len(cuts))
        gain = gain * jnp.repeat(jnp.exp(heights), extent[position] // parts).reshape((-1,) + (1,) * (len(extent) - 1 - position))
    return gain


def normal_values(rng, shape, scale, bound, cuts=(), kind=jnp.bfloat16):
    values = jax.random.normal(rng, shape, jnp.float32) * scale
    if len(cuts) > 0:
        values = block_levels(rng, shape, cuts, -0.22, 0.18) * values
    return jnp.clip(values, min=-bound, max=bound).astype(kind)


def setup_inputs(seed: int = 0) -> dict:
    seeds = jax.random.split(jax.random.key(seed), 8)
    features = normal_values(seeds[0], (MICRO, NODES, D), 1.0, 6.0, ((0, 2), (1, 16)))
    weight = normal_values(seeds[1], (D, D), (D // 4) ** -0.5, 0.25, ((0, 2),))
    bias = normal_values(seeds[2], (D,), 0.5, 3.0, ((0, 2),))
    local_adj = draw_local_adj(jax.random.fold_in(seeds[7], 71), 0)
    send_index = draw_send_index(jax.random.fold_in(seeds[7], 71), 0)
    recv_target = draw_recv_target(jax.random.fold_in(seeds[7], 71), 0)
    cotangent = normal_values(seeds[6], (MICRO, NODES, D), 1.0, 6.0, ((0, 2), (1, 16)))
    return {"features": features, "weight": weight, "bias": bias, "local_adj": local_adj, "send_index": send_index, "recv_target": recv_target, "cotangent": cotangent}


@jax.custom_vjp
def low(v):
    return lax.optimization_barrier(v.astype(jnp.bfloat16)).astype(jnp.float32)

@jax.custom_vjp
def low_back(v):
    return v

def low_keep(v):
    return (low(v), None)

def low_pass(kept, grad):
    return (grad,)

def back_keep(v):
    return (v, None)

def back_low(kept, grad):
    return (low(grad),)
low.defvjp(low_keep, low_pass)
low_back.defvjp(back_keep, back_low)

def one_batch(carry, inputs, weight_full, bias_full):
    feats, neighbours, send_rows, targets, grads_in = inputs
    adjacency = neighbours.astype(jnp.float32).reshape(N_PARTS, PN, PN)
    slots = targets.reshape(N_PARTS, N_PARTS * HALO)
    positions = jnp.arange(PN, dtype=jnp.int32)
    onehot = (slots[:, None, :] == positions[None, :, None]).astype(jnp.float32)
    ratio = 1.0 / (1.0 + lax.optimization_barrier(jnp.sum(adjacency, axis=2)) + lax.optimization_barrier(jnp.sum(onehot, axis=2)))
    source = jnp.arange(N_PARTS, dtype=jnp.int32)[:, None, None] * PN + jnp.maximum(send_rows, 0).astype(jnp.int32)

    def forward(node_feats, weight_val, bias_val):
        blocks = node_feats.reshape(N_PARTS, PN, D)
        sent = low_back(node_feats[source])
        arrived = jnp.transpose(sent, (1, 0, 2, 3)).reshape(N_PARTS, N_PARTS * HALO, D)
        total = jnp.einsum('qij,qjd->qid', adjacency, blocks, precision=lax.Precision.HIGHEST)
        total = total + jnp.einsum('qik,qkd->qid', onehot, arrived, precision=lax.Precision.HIGHEST)
        total = low_back(total + 2.0 * blocks)
        mixed = low(total * ratio[:, :, None]).reshape(NODES, D)
        pre = low_back(jnp.dot(mixed, weight_val, precision=lax.Precision.HIGHEST) + bias_val)
        return jax.nn.gelu(pre, approximate=True)
    outputs, pull = jax.vjp(forward, feats.astype(jnp.float32), weight_full, bias_full)
    dfeats, dweight, dbias = pull(grads_in.astype(jnp.float32))
    return ((carry[0] + dweight, carry[1] + dbias), (outputs.astype(jnp.bfloat16), dfeats.astype(jnp.bfloat16)))

def reference(features, weight, bias, local_adj, send_index, recv_target, cotangent):
    weight_full = weight.astype(jnp.float32)
    bias_full = bias.astype(jnp.float32)
    start = (jnp.zeros((D, D), jnp.float32), jnp.zeros((D,), jnp.float32))
    step_fn = lambda carry, inputs: one_batch(carry, inputs, weight_full, bias_full)
    totals, stacked = lax.scan(step_fn, start, (features, local_adj, send_index, recv_target, cotangent))
    return (stacked[0], stacked[1], totals[0], totals[1])
```

```python
import functools
import math

import jax
import jax.numpy as jnp
from jax import lax
from jax.experimental import pallas as pl
from jax.experimental.pallas import tpu as pltpu
from jax.sharding import PartitionSpec as P

F32 = jnp.float32
BF16 = jnp.bfloat16
AXES = ("parts", "mp")
SWAP = ((0, 1), (1, 0))
GELU_C = math.sqrt(2.0 / math.pi)
GELU_A = 0.044715
CHUNKS = (512, 768, 768)
COSTS = {}
VMEM = pl.BlockSpec(memory_space=pltpu.VMEM)
SMEM = pl.BlockSpec(memory_space=pltpu.SMEM)
ANY = pl.BlockSpec(memory_space=pl.ANY)
HBM = pl.BlockSpec(memory_space=pltpu.HBM)
NT = (((1,), (1,)), ((), ()))


def sds(shape, dtype):
    return jax.ShapeDtypeStruct(shape, dtype)


class Order:
    def __init__(self, limit):
        self.token = None
        self.limit = limit

    def run(self, kernel, name, out_shape, args, scalars=(), far=(), scratch=(), keep=False, limit=None):
        specs = [SMEM] * len(scalars) + [HBM] * len(far) + [VMEM] * len(args)
        args = [*scalars, *far, *args]
        used = len(args)
        aliases = {}
        if keep is not None and keep is not False:
            aliases = {len(args): 0}
            args.append(keep)
            specs.append(ANY)
        if self.token is not None:
            args.append(self.token)
            specs.append(VMEM)
        count, results = len(args), len(out_shape)

        def body(*refs):
            refs[count + results][...] = jnp.zeros((8, 128), F32)
            kernel(*refs[:used], *refs[count : count + results], *refs[count + results + 1 :])

        *out, self.token = pl.pallas_call(
            body,
            name=name,
            in_specs=specs,
            out_specs=((VMEM if keep is False else ANY,) + (VMEM,) * results),
            out_shape=(*out_shape, sds((8, 128), F32)),
            scratch_shapes=scratch,
            input_output_aliases=aliases,
            compiler_params=pltpu.CompilerParams(vmem_limit_bytes=(limit or self.limit) * 2**20),
            cost_estimate=pl.CostEstimate(flops=COSTS.get(name, 1), bytes_accessed=1, transcendentals=0),
        )(*args)
        return out


def hot_rows(index_row, rows):
    match = lax.broadcasted_iota(jnp.int32, (rows, index_row.shape[1]), 0) == index_row
    return jnp.where(match, 1.0, 0.0)


def tiles(width, size=512):
    return [slice(i, min(i + size, width)) for i in range(0, width, size)]


def index_column(index, part, nodes, order=None, turned=0):
    batches, _, depth, parts = index.shape
    slots = batches * parts * depth
    slot = lax.broadcasted_iota(jnp.int32, (slots, parts), 0)
    spot, rest = lax.div(slot, batches * depth), lax.rem(slot, batches * depth)
    if order is not None:
        apart = jnp.zeros((slots, parts), jnp.int32)
        for i, distance in enumerate(order):
            apart = jnp.where(spot == i, distance, apart)
        spot = turn_digits(apart, turned) ^ part
    here = lax.broadcasted_iota(jnp.int32, (slots, parts), 1) == spot
    total = jnp.zeros((slots, parts), jnp.int32)
    for batch in range(batches):
        node = index[batch, 0]
        node = jnp.where(node < 0, -1, node + batch * nodes)
        for h in range(depth):
            total = jnp.where(rest == batch * depth + h, node[h : h + 1], total)
    return jnp.sum(jnp.where(here, total, 0), axis=1, keepdims=True)


def turn_digits(value, turned):
    differ = (value ^ lax.shift_right_logical(value, 1)) & turned
    return value ^ differ ^ (differ << 1)


def as_row(column):
    return jnp.broadcast_to(column, (column.shape[0], 128)).T[:1]


def hot_cols(index_col, cols):
    match = lax.broadcasted_iota(jnp.int32, (index_col.shape[0], cols), 1) == index_col
    return jnp.where(match, 1.0, 0.0)


def outgoing_kernel(nodes, orders, place, feats, adj, send, recv, here, edges, send_row, recv_row, back_row, *rest):
    outs, sems = rest[:-1], rest[-1]
    width = feats.shape[1]
    ranges = tiles(width, width // (sems.shape[0] - 1))
    copies = [pltpu.make_async_copy(feats.at[:, at], here.at[:, at], sems.at[i]) for i, at in enumerate(ranges)]
    copies.append(pltpu.make_async_copy(adj, edges, sems.at[len(ranges)]))
    for copy in copies:
        copy.start()
    me, part = place[0], place[1]
    column = index_column(send, part, nodes, orders[0])
    recv_row[...] = as_row(index_column(recv, part, nodes, orders[1]))
    back_row[...] = as_row(index_column(recv, part, nodes, orders[2], me))
    send_row[...] = as_row(index_column(send, part, nodes, orders[3], me))
    hot = hot_cols(column, feats.shape[0]).astype(BF16)
    size = outs[0].shape[0]
    for at, copy in zip(ranges, copies):
        copy.wait()
        value = jnp.dot(hot, here[:, at], preferred_element_type=F32)
        for i, out in enumerate(outs):
            out[:, at] = value[i * size : (i + 1) * size].astype(BF16)
    copies[-1].wait()


def regroup_kernel(size, orders, *refs):
    pieces, outs = refs[: -len(orders)], refs[-len(orders) :]
    values = [piece[...].astype(F32) for piece in pieces]
    for order, out in zip(orders, outs):
        blocks = [values[i][block * size : (block + 1) * size] for i, block in order]
        out[...] = jnp.concatenate(blocks, axis=0).astype(BF16)


def stack(pieces):
    return jnp.concatenate([piece[...] for piece in pieces], axis=0)


def mix_kernel(weight, adj, recv_row, feats, mixed, mixed_t, ratio, ratio_row, adj_t, own, sem):
    copy = pltpu.make_async_copy(weight, own, sem)
    copy.start()
    batches, nodes, _ = adj.shape
    half = mixed.shape[2]
    eye = lax.broadcasted_iota(jnp.int32, (nodes, nodes), 0) == lax.broadcasted_iota(
        jnp.int32, (nodes, nodes), 1
    )
    for batch in range(batches):
        here = slice(batch * nodes, (batch + 1) * nodes)
        count = adj[batch].astype(F32)
        hot = hot_rows(recv_row[...] - batch * nodes, nodes)
        degree = jnp.sum(count, axis=1, keepdims=True) + jnp.sum(hot, axis=1, keepdims=True)
        scale = 1.0 / (1.0 + degree)
        ratio[here] = scale
        ratio_row[:, here] = jnp.broadcast_to(scale, (nodes, 128)).T[:8]
        count = count + jnp.where(eye, 2.0, 0.0)
        adj_t[batch] = count.T.astype(BF16)
        count = count.astype(BF16)
        for at in tiles(feats.shape[1]):
            value = scale * jnp.dot(count, feats[here, at], preferred_element_type=F32)
            low = at.start % half
            mixed[at.start // half, here, low : low + at.stop - at.start] = value.astype(BF16)
            mixed_t[at, here] = value.T.astype(BF16)
    copy.wait()


def pre_own_kernel(place, away, mixed, weight, pre, other, sem):
    copy = pltpu.make_async_copy(away, other, sem)
    copy.start()
    me = place[0]
    for at in tiles(pre.shape[1]):
        pre[:, at] = jnp.dot(mixed[me], weight[:, at], preferred_element_type=F32)
    copy.wait()


def pre_other_kernel(place, before, mixed, weight, bias_own, bias_other, pre):
    me = place[0]
    half = weight.shape[0]
    first = me == 0
    mine, theirs = bias_own[...].astype(F32), bias_other[...].astype(F32)
    bias = (jnp.where(first, mine, theirs), jnp.where(first, theirs, mine))
    for at in tiles(pre.shape[1]):
        total = before[:, at] + jnp.dot(mixed[1 - me], weight[:, at], preferred_element_type=F32)
        low = at.start % half
        pre[:, at] = total + bias[at.start // half][:, low : low + at.stop - at.start]


def finish_kernel(axes, block, place, recv_row, ratio_row, mixed_t, *refs):
    pieces, (mine, theirs) = refs[:-2], refs[-2:]
    me, part = place[0], place[1]
    first = me == 0
    rows = mixed_t.shape[1]
    hot = hot_rows(recv_row[...], rows).T.astype(BF16)
    scale = ratio_row[0:1]
    for at in tiles(mixed_t.shape[0], 256):
        remote = jnp.dot(stack([piece.at[:, at] for piece in pieces]).T, hot, preferred_element_type=F32)
        value = (mixed_t[at].astype(F32) + scale * remote).reshape(128 // block, 2, block, rows)
        for out, swap in ((mine, False), (theirs, True)):
            low, high = (1, 0) if swap else (0, 1)
            chosen = jnp.where(first, value[:, low], value[:, high])
            if axes is None:
                out[at.start // 2 : at.stop // 2] = chosen.reshape(128, rows).astype(BF16)
                continue
            owner = 1 - me if swap else me
            for i in range(128 // block):
                spot = spot_of(axes, part, owner, at.start // (2 * block) + i)
                out[pl.ds(pl.multiple_of(spot * block, block), block)] = chosen[i].astype(BF16)


def remote_kernel(place, own, other, *refs):
    pieces, out = refs[:-1], refs[-1]
    half = own.shape[0]
    me = place[0]
    spots = out.shape[0] // 2
    here = stack([piece.at[:, pl.ds(pl.multiple_of(me * half, half), half)] for piece in pieces])
    there = stack([piece.at[:, pl.ds(pl.multiple_of((1 - me) * half, half), half)] for piece in pieces])
    for at in tiles(own.shape[1]):
        product = jnp.dot(here, own[:, at], preferred_element_type=F32)
        product += jnp.dot(there, other[:, at], preferred_element_type=F32)
        high = product.astype(BF16)
        out[:spots, at] = high
        out[spots:, at] = (product - high.astype(F32)).astype(BF16)


def gelu_kernel(start, recv_row, ratio, remote, pre, cot, act, dpre, bias_term, value, result, sems):
    rows, size = dpre.shape
    at = slice(start, start + size)
    hot = hot_rows(recv_row[...], rows).astype(BF16)
    value[...] = pre[:, at] + ratio[...] * jnp.dot(
        jnp.concatenate([hot, hot], axis=1), remote[:, at], preferred_element_type=F32
    )
    step = 64

    def body(i, total):
        here = pl.ds(pl.multiple_of(i * step, step), step)
        v = value[here]
        square = v * v
        left = 0.5 + 0.5 * jnp.tanh(v * (GELU_C + GELU_C * GELU_A * square))
        out = v * left
        result[here] = out.astype(BF16)
        slope = left + (out - out * left) * (2.0 * GELU_C + 6.0 * GELU_C * GELU_A * square)
        grad = (cot[here, at].astype(F32) * slope).astype(BF16)
        dpre[here] = grad
        return total + grad.astype(F32).reshape(step // 8, 8, size).sum(axis=0)

    total = jnp.zeros((8, size), F32)
    pieces = sems.shape[0]
    steps = rows // step
    copies = []
    for piece in range(pieces):
        low, high = piece * steps // pieces, (piece + 1) * steps // pieces
        total = lax.fori_loop(low, high, body, total)
        here = slice(low * step, high * step)
        copies.append(pltpu.make_async_copy(result.at[here], act.at[here, at], sems.at[piece]))
        copies[-1].start()
    bias_term[...] = jnp.sum(total, axis=0, keepdims=True)
    for copy in copies:
        copy.wait()


def spot_of(axes, part, owner, index):
    apart = turn_digits(part ^ index, owner)
    spot = 0
    for axis in axes:
        spot = spot * 2 + (lax.shift_right_logical(apart, axis) & 1)
    return spot


def grad_kernel(order, block, mine, theirs, dpre_mine, dpre_theirs, keep, leave):
    half = keep.shape[0]
    count = min(256 // block, len(order) // 2)
    for i in range(0, len(order), count):
        spots = [slice(spot * block, (spot + 1) * block) for spot in order[i : i + count]]
        total = jnp.dot(stack([mine.at[at] for at in spots]), dpre_mine[...], preferred_element_type=F32)
        total += jnp.dot(stack([theirs.at[at] for at in spots]), dpre_theirs[...], preferred_element_type=F32)
        low = i * block % half
        out = keep if i * block < half else leave
        out[low : low + count * block] = total.astype(BF16)


def sent_kernel(chunks, parts, per_part, sources, place, recv_row, ratio_row, own, other, *refs):
    dpres, bias_terms, outs = refs[:chunks], refs[chunks : 2 * chunks], refs[2 * chunks : -1]
    lines = refs[-1]
    half, width = own.shape
    rows = ratio_row.shape[1]
    hot = (hot_rows(recv_row[...], rows).T * ratio_row[0:1]).astype(BF16)
    grad = jnp.concatenate(
        [jnp.dot(hot, dpre[...], preferred_element_type=F32).astype(BF16) for dpre in dpres], axis=1
    )
    me, part = place[0], place[1]
    size = outs[0].shape[0]
    for weight, spot in ((own, me), (other, 1 - me)):
        for at in tiles(half, 256):
            value = lax.dot_general(grad, weight[at], NT, preferred_element_type=F32)
            for i, out in enumerate(outs):
                here = pl.ds(pl.multiple_of(spot * half + at.start, 256), 256)
                out[:, here] = value[i * size : (i + 1) * size].astype(BF16)
    bias = jnp.concatenate([term[...] for term in bias_terms], axis=1)
    high = bias.astype(BF16).astype(F32)
    middle = (bias - high).astype(BF16).astype(F32)
    line = lax.broadcasted_iota(jnp.int32, (8, width), 0)
    lines[...] = jnp.where(line == 0, high, jnp.where(line == 1, middle, bias - high - middle))
    count = width // parts
    line = lax.broadcasted_iota(jnp.int32, (8, count), 0)
    for i, out in enumerate(outs):
        pieces = []
        for source in sources[i]:
            if len(outs) > 1:
                to = part ^ turn_digits(source, me)
                piece = lines[:, pl.ds(pl.multiple_of(to * count, count), count)]
            else:
                piece = lines[:, source * count : (source + 1) * count]
            piece = jnp.where(line < 3, piece, 0.0)
            if count < 128:
                piece = jnp.concatenate([piece, jnp.zeros((8, 128 - count), F32)], axis=1)
            if per_part > 8:
                piece = jnp.concatenate([piece, jnp.zeros((per_part - 8, piece.shape[1]), F32)], axis=0)
            pieces.append(piece)
        out[:, width:] = jnp.concatenate(pieces, axis=0).astype(BF16)


def back_kernel(chunks, ratio, weight, *refs):
    dpres, out = refs[:chunks], refs[chunks]
    for at in tiles(weight.shape[0], 256):
        total = None
        start = 0
        for dpre in dpres:
            size = dpre.shape[1]
            term = lax.dot_general(dpre[...], weight[at, start : start + size], NT, preferred_element_type=F32)
            total = term if total is None else total + term
            start += size
        out[:, at] = (ratio[...] * total).astype(BF16)


def local_kernel(adj_t, dtotal, out):
    batches, nodes, _ = adj_t.shape
    for batch in range(batches):
        here = slice(batch * nodes, (batch + 1) * nodes)
        for at in tiles(dtotal.shape[1]):
            out[here, at] = jnp.dot(adj_t[batch], dtotal[here, at], preferred_element_type=F32)


def input_kernel(place, send_row, own, other, *refs):
    pieces, (out, bias_out) = refs[:-2], refs[-2:]
    rows, half = own.shape
    hot = hot_rows(send_row[...], rows).astype(BF16)
    me = place[0]
    for partial, spot in ((own, me), (other, 1 - me)):
        for at in tiles(half):
            here = pl.ds(pl.multiple_of(spot * half + at.start, 512), at.stop - at.start)
            total = partial[:, at] + jnp.dot(hot, stack([piece.at[:, here] for piece in pieces]), preferred_element_type=F32)
            out[:, here] = total.astype(BF16)
    bias_out[...] = sum(jnp.sum(piece[:, 2 * half :].astype(F32), axis=0, keepdims=True) for piece in pieces)


def halve_kernel(keep, arrived, stay, leave):
    half = stay.shape[0]
    for out, low in ((leave, half), (stay, 0)):
        at = slice(low, low + half)
        out[...] = (keep[at].astype(F32) + arrived[at].astype(F32)).astype(BF16)


def last_kernel(*refs):
    out = refs[-1]
    start = 0
    for keep, arrived in zip(refs[:-1:2], refs[1:-1:2]):
        size = keep.shape[1]
        out[:, start : start + size] = keep[...].astype(F32) + arrived[...].astype(F32)
        start += size


def partners(parts, axis):
    turned = {0: 1, 1: 0}.get(axis, axis) if parts > 2 else axis
    return [(p * 2 + c, (p ^ (1 << (axis, turned)[c])) * 2 + c) for p in range(parts) for c in range(2)]


class Reduction:
    def __init__(self, order, parts, axes, keep, leave):
        self.order = order
        self.parts = parts
        self.axes = list(axes)
        self.keep = keep
        self.send(leave)

    def send(self, leave):
        self.arrived = lax.ppermute(leave, AXES, partners(self.parts, self.axes.pop(0)))

    def step(self):
        rows, size = self.keep.shape
        half = sds((rows // 2, size), BF16)
        self.keep, leave = self.order.run(halve_kernel, "halve", (half, half), (self.keep, self.arrived))
        self.send(leave)


class Exchange:
    def __init__(self, order, parts, axes, size, pieces):
        self.order, self.parts, self.axes, self.size = order, parts, list(axes), size
        self.lists = halves(range(parts), self.axes[0])
        self.stay, leave = pieces
        self.arrived = lax.ppermute(leave, AXES, partners(parts, self.axes.pop(0)))

    def step(self):
        if not self.axes:
            return
        found = {r: (i, spot) for i in range(2) for spot, r in enumerate(self.lists[i])}
        axis = self.axes.pop(0)
        self.lists = halves(self.lists[0] + self.lists[1], axis)
        orders = [[found[r] for r in part] for part in self.lists]
        shape = sds(self.stay.shape, BF16)
        self.stay, leave = self.order.run(
            functools.partial(regroup_kernel, self.size, orders), "regroup", (shape, shape), (self.stay, self.arrived)
        )
        self.arrived = lax.ppermute(leave, AXES, partners(self.parts, axis))


def halves(distances, axis):
    return [[r for r in distances if (r >> axis) & 1 == side] for side in range(2)]


def local(parts, features, weight, bias, local_adj, send_index, recv_target, cotangent):
    batches, nodes, width = features.shape
    rows = batches * nodes
    half = width // 2
    core = lax.axis_index("mp").astype(jnp.int32)
    part = lax.axis_index("parts").astype(jnp.int32)
    place = jnp.stack([core, part])
    paired = parts & (parts - 1) == 0 and width % (2 * parts) == 0 and (width // (2 * parts)) % 16 == 0
    block = width // (2 * parts)

    feats = features.reshape(rows, width)
    cot = cotangent.reshape(rows, width)
    digits = parts.bit_length() - 1
    near = min(4, parts)
    far = parts // near
    orders = [None] * 4
    early = late = None
    if paired:
        late = list(range(digits))
        early = late[2:] + late[:2]
        back = late[:1:-1] + late[:2]
        first, last = halves(range(parts), back[0]), list(range(parts))
        for axis in back:
            last = sum(halves(last, axis), [])
        orders = [list(range(parts)), [k * near + j for j in range(near) for k in range(far)], sum(first, []), last]
    slots = send_index.size
    per_part = slots // parts

    def move(pieces, stride):
        moved = [pieces[0]]
        for i in range(1, len(pieces)):
            perm = [(p, p ^ (i * stride)) for p in range(parts)]
            moved.append(lax.ppermute(pieces[i], "parts", perm))
        return moved

    def exchange(values):
        moved = lax.all_to_all(
            values.reshape(parts, per_part, values.shape[1]), "parts", split_axis=0, concat_axis=0, tiled=True
        )
        return moved.reshape(values.shape)

    other = lax.ppermute(weight, "mp", SWAP)
    bias_own = bias.reshape(1, half)
    bias_other = lax.ppermute(bias_own, "mp", SWAP)
    order = Order(12 if paired else 48)
    run = order.run
    turn = (0, 1, 3, 2)
    pieces = far if paired else 1
    row = sds((1, slots), jnp.int32)
    feats, local_adj, send_row, recv_row, back_row, *outgoing = run(
        functools.partial(outgoing_kernel, nodes, orders),
        "outgoing",
        (sds((rows, width), BF16), sds(local_adj.shape, jnp.int32), row, row, row)
        + (sds((slots // pieces, width), BF16),) * pieces,
        (jnp.transpose(send_index, turn), jnp.transpose(recv_target, turn)),
        scalars=(place,),
        far=(feats, local_adj),
        scratch=[pltpu.SemaphoreType.DMA((5,))],
        limit=47,
    )
    if paired:
        outgoing = move(outgoing, near)

    mixed, mixed_t, ratio, ratio_row, adj_t, weight = run(
        mix_kernel,
        "mix",
        (
            sds((2, rows, half), BF16),
            sds((width, rows), BF16),
            sds((rows, 1), F32),
            sds((8, rows), F32),
            sds((batches, nodes, nodes), BF16),
            sds(weight.shape, BF16),
        ),
        (local_adj, recv_row, feats),
        far=(weight,),
        scratch=[pltpu.SemaphoreType.DMA(())],
        limit=36,
    )
    if paired:
        arrived = run(
            functools.partial(
                regroup_kernel, per_part, [[(k, j) for k in range(far)] for j in range(near)]
            ),
            "regroup",
            (sds((far * per_part, width), BF16),) * near,
            outgoing,
        )
        arrived = move(arrived, 1)
    else:
        arrived = [exchange(outgoing[0])]
    pre, other = run(
        pre_own_kernel,
        "pre_own",
        (sds((rows, width), F32), sds(other.shape, BF16)),
        (mixed, weight),
        scalars=(place,),
        far=(other,),
        scratch=[pltpu.SemaphoreType.DMA(())],
    )
    (pre,) = run(
        pre_other_kernel,
        "pre_other",
        (sds((rows, width), F32),),
        (pre, mixed, other, bias_own, bias_other),
        scalars=(place,),
    )
    (remote,) = run(
        remote_kernel,
        "remote_product",
        (sds((2 * slots, width), BF16),),
        (weight, other, *arrived),
        scalars=(place,),
    )

    starts = [sum(CHUNKS[:i]) for i in range(len(CHUNKS))]
    act = None
    dpres, dpres_other, bias_terms, sums = [], [], [], []

    def gelu(i):
        nonlocal act
        size = CHUNKS[i]
        act, dpre, bias_term = run(
            functools.partial(gelu_kernel, starts[i]),
            "gelu",
            (sds((rows, width), BF16), sds((rows, size), BF16), sds((1, size), F32)),
            (recv_row, ratio, remote, pre, cot),
            scratch=[pltpu.VMEM((rows, size), F32), pltpu.VMEM((rows, size), BF16), pltpu.SemaphoreType.DMA((3,))],
            keep=act,
        )
        dpres.append(dpre)
        dpres_other.append(lax.ppermute(dpre, "mp", SWAP))
        bias_terms.append(bias_term)

    def grad(i):
        size = CHUNKS[i]
        shape = sds((half // 2, size), BF16)
        if paired:
            axes = early if i == 0 else late
            spots = [sum(((r >> axes[::-1].index(axis)) & 1) << d for d, axis in enumerate(late[::-1])) for r in range(parts)]
            size_of = block
        else:
            spots, size_of = list(range(half // 128)), 128
        keep, leave = run(
            functools.partial(grad_kernel, spots, size_of),
            "grad",
            (shape, shape),
            (mine, theirs, dpres[i], dpres_other[i]),
        )
        if paired:
            sums.append(Reduction(order, parts, axes, keep, leave))
            return
        both = jnp.concatenate([keep, leave]).astype(F32)
        sums.append(lax.psum_scatter(both, "parts", scatter_dimension=0, tiled=True))

    def step(i):
        if paired:
            sums[i].step()

    def back_half(matrix):
        (dtotal,) = run(back_kernel_of, "back", (sds((rows, half), BF16),), (ratio, matrix, *dpres))
        return dtotal

    def around(dtotal):
        (partial,) = run(local_kernel, "input_local", (sds((rows, half), F32),), (adj_t, dtotal))
        return partial

    back_kernel_of = functools.partial(back_kernel, len(CHUNKS))

    mine, theirs = run(
        functools.partial(finish_kernel, late, block),
        "finish_mixed",
        (sds((half, rows), BF16), sds((half, rows), BF16)),
        (recv_row, ratio_row, mixed_t, *arrived),
        scalars=(place,),
    )
    theirs = lax.ppermute(theirs, "mp", SWAP)
    for i in range(len(CHUNKS)):
        gelu(i)
    grad(0)
    grad(1)

    extra = max(128, width // parts)
    pieces = 2 if paired else 1
    sent = run(
        functools.partial(
            sent_kernel, len(CHUNKS), parts, per_part, first if paired else [list(range(parts))]
        ),
        "sent_grads",
        (sds((slots // pieces, width + extra), BF16),) * pieces,
        (back_row, ratio_row, weight, other, *dpres, *bias_terms),
        scalars=(place,),
        scratch=[pltpu.VMEM((8, width), F32)],
    )
    if paired:
        swap = Exchange(order, parts, back, per_part, sent)
    else:
        returned = [exchange(sent[0])]

    def pass_on():
        if paired:
            swap.step()

    grad(2)
    step(0)
    step(1)
    pass_on()
    dtotal_own = back_half(weight)
    step(2)
    dtotal_other = back_half(other)
    step(0)
    step(1)
    pass_on()
    partial_own = around(dtotal_own)
    step(2)
    partial_other = around(dtotal_other)
    step(0)
    step(1)
    pass_on()
    step(2)
    if paired:
        returned = [swap.stay, swap.arrived]
    input_grad, bias_all = run(
        input_kernel,
        "input_gradient",
        (sds((rows, width), BF16), sds((1, extra), F32)),
        (send_row, partial_own, partial_other, *returned),
        scalars=(place,),
    )
    if paired:
        (weight_grad,) = run(
            last_kernel, "last_sum", (sds((block, width), F32),), [x for s in sums for x in (s.keep, s.arrived)]
        )
    else:
        weight_grad = jnp.concatenate(sums, axis=1)
    bias_all = bias_all + lax.ppermute(bias_all, "mp", SWAP)
    count = width // (2 * parts)
    bias_grad = jnp.where(core == 0, bias_all[0, :count], bias_all[0, count : 2 * count])
    return (
        act.reshape(batches, nodes, width),
        input_grad.reshape(batches, nodes, width),
        weight_grad,
        bias_grad,
    )


def solution(mesh):
    return jax.shard_map(
        functools.partial(local, mesh.shape["parts"]),
        mesh=mesh,
        in_specs=(
            P("mp", "parts", None),
            P("mp", None),
            P("mp"),
            P("mp", "parts", None),
            P("mp", "parts", None, None),
            P("mp", "parts", None, None),
            P("mp", "parts", None),
        ),
        out_specs=(
            P("mp", "parts", None),
            P("mp", "parts", None),
            P(("parts", "mp"), None),
            P(("parts", "mp")),
        ),
        check_vma=False,
    )
```

```python
import functools
import math

import jax
import jax.numpy as jnp
from jax import lax
from jax.experimental import pallas as pl
from jax.experimental.pallas import tpu as pltpu
from jax.sharding import PartitionSpec as P

F32 = jnp.float32
BF16 = jnp.bfloat16
AXES = ("parts", "mp")
SWAP = ((0, 1), (1, 0))
GELU_C = math.sqrt(2.0 / math.pi)
GELU_A = 0.044715
CHUNKS = (1024, 768, 256)
FAR_FIRST = 2
BACK = (3, 2, 0, 1)
DIRECT = True
JOIN = False
PLAN = ('f', 'g0', 'g1', 'g2', 's', 'd0', 'd1', 'd2', 'e', 'r0', 'b0', 'r2', 'r1', 'r0', 'b1', 'l0', 'r1', 'r2', 'r0', 'r2', 'r1', 'l1', 'i')
COSTS = (1, 1000000000, 4000000000, 1, 8000000000, 16000000000, 1, 1, 4000000000, 1, 1, 4000000000, 2000000000, 4000000000, 1000000000, 1, 1, 1000000000, 1, 1, 1, 1, 1)
VMEM = pl.BlockSpec(memory_space=pltpu.VMEM)
SMEM = pl.BlockSpec(memory_space=pltpu.SMEM)
ANY = pl.BlockSpec(memory_space=pl.ANY)
HBM = pl.BlockSpec(memory_space=pltpu.HBM)
NT = (((1,), (1,)), ((), ()))


def sds(shape, dtype):
    return jax.ShapeDtypeStruct(shape, dtype)


class Order:
    def __init__(self, limit):
        self.token = None
        self.limit = limit
        self.cost = 1

    def run(self, kernel, name, out_shape, args, scalars=(), far=(), scratch=(), keep=False):
        specs = [SMEM] * len(scalars) + [HBM] * len(far) + [VMEM] * len(args)
        args = [*scalars, *(pltpu.with_memory_space_constraint(x, pltpu.HBM) for x in far), *args]
        used = len(args)
        aliases = {}
        if keep is not None and keep is not False:
            aliases = {len(args): 0}
            args.append(keep)
            specs.append(ANY)
        if self.token is not None:
            args.append(self.token)
            specs.append(VMEM)
        count, results = len(args), len(out_shape)

        def body(*refs):
            refs[count + results][...] = jnp.zeros((8, 128), F32)
            kernel(*refs[:used], *refs[count : count + results], *refs[count + results + 1 :])

        *out, self.token = pl.pallas_call(
            body,
            name=name,
            in_specs=specs,
            out_specs=((VMEM if keep is False else ANY,) + (VMEM,) * results),
            out_shape=(*out_shape, sds((8, 128), F32)),
            scratch_shapes=scratch,
            input_output_aliases=aliases,
            compiler_params=pltpu.CompilerParams(vmem_limit_bytes=self.limit * 2**20),
            cost_estimate=pl.CostEstimate(flops=self.cost, bytes_accessed=1, transcendentals=0),
        )(*args)
        return out


def hot_rows(index_row, rows):
    match = lax.broadcasted_iota(jnp.int32, (rows, index_row.shape[1]), 0) == index_row
    return jnp.where(match, 1.0, 0.0)


def tiles(width, size=512):
    return [slice(i, min(i + size, width)) for i in range(0, width, size)]


def index_column(index, part, nodes, order=None, turned=0):
    batches, _, depth, parts = index.shape
    slots = batches * parts * depth
    slot = lax.broadcasted_iota(jnp.int32, (slots, parts), 0)
    spot, rest = lax.div(slot, batches * depth), lax.rem(slot, batches * depth)
    if order is not None:
        apart = jnp.zeros((slots, parts), jnp.int32)
        for i, distance in enumerate(order):
            apart = jnp.where(spot == i, distance, apart)
        spot = turn_digits(apart, turned) ^ part
    here = lax.broadcasted_iota(jnp.int32, (slots, parts), 1) == spot
    total = jnp.zeros((slots, parts), jnp.int32)
    for batch in range(batches):
        node = index[batch, 0]
        node = jnp.where(node < 0, -1, node + batch * nodes)
        for h in range(depth):
            total = jnp.where(rest == batch * depth + h, node[h : h + 1], total)
    return jnp.sum(jnp.where(here, total, 0), axis=1, keepdims=True)


def turn_digits(value, turned):
    differ = (value ^ lax.shift_right_logical(value, 1)) & turned
    return value ^ differ ^ (differ << 1)


def as_row(column):
    return jnp.broadcast_to(column, (column.shape[0], 128)).T[:1]


def hot_cols(index_col, cols):
    match = lax.broadcasted_iota(jnp.int32, (index_col.shape[0], cols), 1) == index_col
    return jnp.where(match, 1.0, 0.0)


def outgoing_kernel(nodes, order, place, feats, send_far, here, *rest):
    outs, (send, sems) = rest[:-2], rest[-2:]
    width = feats.shape[1]
    ranges = tiles(width, width // (sems.shape[0] - 1))
    copies = [pltpu.make_async_copy(feats.at[:, at], here.at[:, at], sems.at[i]) for i, at in enumerate(ranges)]
    fetch = pltpu.make_async_copy(send_far, send, sems.at[len(ranges)])
    for copy in (fetch, *copies):
        copy.start()
    fetch.wait()
    hot = hot_cols(index_column(send, place[1], nodes, order), feats.shape[0]).astype(BF16)
    size = outs[0].shape[0]
    for at, copy in zip(ranges, copies):
        copy.wait()
        value = jnp.dot(hot, here[:, at], preferred_element_type=F32)
        for i, out in enumerate(outs):
            out[:, at] = value[i * size : (i + 1) * size].astype(BF16)


def regroup_kernel(size, orders, *refs):
    pieces, outs = refs[: -len(orders)], refs[-len(orders) :]
    values = [piece[...].astype(F32) for piece in pieces]
    for order, out in zip(orders, outs):
        blocks = [values[i][block * size : (block + 1) * size] for i, block in order]
        out[...] = jnp.concatenate(blocks, axis=0).astype(BF16)


def stack(pieces):
    return jnp.concatenate([piece[...] for piece in pieces], axis=0)


def mix_kernel(orders, place, weight, edges, send_far, recv_far, feats, *refs):
    mixed, mixed_t, ratio, ratio_row, adj_t, own, send_row, recv_row, back_row, adj, send, recv, sems = refs
    copies = [
        pltpu.make_async_copy(source, target, sems.at[i])
        for i, (source, target) in enumerate(((recv_far, recv), (send_far, send), (edges, adj), (weight, own)))
    ]
    for copy in copies:
        copy.start()
    for copy in copies[:3]:
        copy.wait()
    me, part = place[0], place[1]
    nodes = adj.shape[1]
    recv_row[...] = as_row(index_column(recv, part, nodes, orders[1]))
    back_row[...] = as_row(index_column(recv, part, nodes, orders[2], 0 if DIRECT else me))
    send_row[...] = as_row(index_column(send, part, nodes, orders[3], 0 if DIRECT else me))
    batches, nodes, _ = adj.shape
    half = mixed.shape[2]
    eye = lax.broadcasted_iota(jnp.int32, (nodes, nodes), 0) == lax.broadcasted_iota(
        jnp.int32, (nodes, nodes), 1
    )
    for batch in range(batches):
        here = slice(batch * nodes, (batch + 1) * nodes)
        count = adj[batch].astype(F32)
        hot = hot_rows(recv_row[...] - batch * nodes, nodes)
        degree = jnp.sum(count, axis=1, keepdims=True) + jnp.sum(hot, axis=1, keepdims=True)
        scale = 1.0 / (1.0 + degree)
        ratio[here] = scale
        ratio_row[:, here] = jnp.broadcast_to(scale, (nodes, 128)).T[:8]
        count = count + jnp.where(eye, 2.0, 0.0)
        adj_t[batch] = count.T.astype(BF16)
        count = count.astype(BF16)
        for at in tiles(feats.shape[1]):
            value = scale * jnp.dot(count, feats[here, at], preferred_element_type=F32)
            low = at.start % half
            mixed[at.start // half, here, low : low + at.stop - at.start] = value.astype(BF16)
            mixed_t[at, here] = value.T.astype(BF16)
    copies[3].wait()


def pre_own_kernel(place, away, mixed, weight, pre, other, sem):
    copy = pltpu.make_async_copy(away, other, sem)
    copy.start()
    me = place[0]
    for at in tiles(pre.shape[1]):
        pre[:, at] = jnp.dot(mixed[me], weight[:, at], preferred_element_type=F32)
    copy.wait()


def pre_other_kernel(place, before, mixed, weight, pre):
    me = place[0]
    for at in tiles(pre.shape[1]):
        pre[:, at] = before[:, at] + jnp.dot(mixed[1 - me], weight[:, at], preferred_element_type=F32)


def finish_kernel(axes, block, place, recv_row, ratio_row, mixed_t, *refs):
    pieces, (mine, theirs) = refs[:-2], refs[-2:]
    me, part = place[0], place[1]
    first = me == 0
    rows = mixed_t.shape[1]
    hot = hot_rows(recv_row[...], rows).T.astype(BF16)
    scale = ratio_row[0:1]
    for at in tiles(mixed_t.shape[0], 256):
        remote = jnp.dot(stack([piece.at[:, at] for piece in pieces]).T, hot, preferred_element_type=F32)
        value = (mixed_t[at].astype(F32) + scale * remote).reshape(128 // block, 2, block, rows)
        for out, swap in ((mine, False), (theirs, True)):
            low, high = (1, 0) if swap else (0, 1)
            chosen = jnp.where(first, value[:, low], value[:, high])
            if axes is None:
                out[at.start // 2 : at.stop // 2] = chosen.reshape(128, rows).astype(BF16)
                continue
            owner = 1 - me if swap else me
            for i in range(128 // block):
                spot = spot_of(axes, part, owner, at.start // (2 * block) + i)
                out[pl.ds(pl.multiple_of(spot * block, block), block)] = chosen[i].astype(BF16)


def remote_kernel(place, own, other, bias_own, bias_other, *refs):
    pieces, (out, bias) = refs[:-2], refs[-2:]
    half = own.shape[0]
    me = place[0]
    spots = out.shape[0] // 2
    here = stack([piece.at[:, pl.ds(pl.multiple_of(me * half, half), half)] for piece in pieces])
    there = stack([piece.at[:, pl.ds(pl.multiple_of((1 - me) * half, half), half)] for piece in pieces])
    for at in tiles(own.shape[1]):
        product = jnp.dot(here, own[:, at], preferred_element_type=F32)
        product += jnp.dot(there, other[:, at], preferred_element_type=F32)
        high = product.astype(BF16)
        out[:spots, at] = high
        out[spots:, at] = (product - high.astype(F32)).astype(BF16)
    mine, theirs = bias_own[...].astype(F32), bias_other[...].astype(F32)
    bias[:, :half] = jnp.where(me == 0, mine, theirs)
    bias[:, half:] = jnp.where(me == 0, theirs, mine)


def gelu_kernel(start, recv_row, ratio, remote, pre, bias, cot, act, dpre, bias_term, value, result, sems):
    rows, size = dpre.shape
    at = slice(start, start + size)
    hot = hot_rows(recv_row[...], rows).astype(BF16)
    value[...] = pre[:, at] + bias[:, at] + ratio[...] * jnp.dot(
        jnp.concatenate([hot, hot], axis=1), remote[:, at], preferred_element_type=F32
    )
    step = 64

    def body(i, total):
        here = pl.ds(pl.multiple_of(i * step, step), step)
        v = value[here]
        square = v * v
        left = 0.5 + 0.5 * jnp.tanh(v * (GELU_C + GELU_C * GELU_A * square))
        out = v * left
        result[here] = out.astype(BF16)
        slope = left + (out - out * left) * (2.0 * GELU_C + 6.0 * GELU_C * GELU_A * square)
        grad = (cot[here, at].astype(F32) * slope).astype(BF16)
        dpre[here] = grad
        return total + grad.astype(F32).reshape(step // 8, 8, size).sum(axis=0)

    total = jnp.zeros((8, size), F32)
    pieces = sems.shape[0]
    steps = rows // step
    copies = []
    for piece in range(pieces):
        low, high = piece * steps // pieces, (piece + 1) * steps // pieces
        total = lax.fori_loop(low, high, body, total)
        here = slice(low * step, high * step)
        copies.append(pltpu.make_async_copy(result.at[here], act.at[here, at], sems.at[piece]))
        copies[-1].start()
    bias_term[...] = jnp.sum(total, axis=0, keepdims=True)
    for copy in copies:
        copy.wait()


def spot_of(axes, part, owner, index):
    apart = turn_digits(part ^ index, owner)
    spot = 0
    for axis in axes:
        spot = spot * 2 + (lax.shift_right_logical(apart, axis) & 1)
    return spot


def grad_kernel(order, block, mine, theirs, dpre_mine, dpre_theirs, keep, leave):
    half = keep.shape[0]
    count = min(256 // block, len(order) // 2)
    for i in range(0, len(order), count):
        spots = [slice(spot * block, (spot + 1) * block) for spot in order[i : i + count]]
        total = jnp.dot(stack([mine.at[at] for at in spots]), dpre_mine[...], preferred_element_type=F32)
        total += jnp.dot(stack([theirs.at[at] for at in spots]), dpre_theirs[...], preferred_element_type=F32)
        low = i * block % half
        out = keep if i * block < half else leave
        out[low : low + count * block] = total.astype(BF16)


def sent_kernel(chunks, parts, per_part, sources, place, recv_row, ratio_row, *refs):
    dpres, bias_terms, outs = refs[:chunks], refs[chunks : 2 * chunks], refs[2 * chunks : -1]
    lines = refs[-1]
    width = lines.shape[1]
    rows = ratio_row.shape[1]
    hot = (hot_rows(recv_row[...], rows).T * ratio_row[0:1]).astype(BF16)
    me, part = place[0], place[1]
    size = outs[0].shape[0]
    start = 0
    for dpre in dpres:
        at = slice(start, start + dpre.shape[1])
        value = jnp.dot(hot, dpre[...], preferred_element_type=F32)
        for i, out in enumerate(outs):
            out[:, at] = value[i * size : (i + 1) * size].astype(BF16)
        start = at.stop
    bias = jnp.concatenate([term[...] for term in bias_terms], axis=1)
    high = bias.astype(BF16).astype(F32)
    middle = (bias - high).astype(BF16).astype(F32)
    line = lax.broadcasted_iota(jnp.int32, (8, width), 0)
    lines[...] = jnp.where(line == 0, high, jnp.where(line == 1, middle, bias - high - middle))
    count = width // parts
    line = lax.broadcasted_iota(jnp.int32, (8, count), 0)
    for i, out in enumerate(outs):
        pieces = []
        for source in sources[i]:
            if len(outs) > 1:
                to = part ^ turn_digits(source, 0 if DIRECT else me)
                piece = lines[:, pl.ds(pl.multiple_of(to * count, count), count)]
            else:
                piece = lines[:, source * count : (source + 1) * count]
            piece = jnp.where(line < 3, piece, 0.0)
            if count < 128:
                piece = jnp.concatenate([piece, jnp.zeros((8, 128 - count), F32)], axis=1)
            if per_part > 8:
                piece = jnp.concatenate([piece, jnp.zeros((per_part - 8, piece.shape[1]), F32)], axis=0)
            pieces.append(piece)
        out[:, width:] = jnp.concatenate(pieces, axis=0).astype(BF16)


def back_kernel(chunks, ratio, weight, *refs):
    dpres, out = refs[:chunks], refs[chunks]
    for at in tiles(weight.shape[0], 256):
        total = None
        start = 0
        for dpre in dpres:
            size = dpre.shape[1]
            term = lax.dot_general(dpre[...], weight[at, start : start + size], NT, preferred_element_type=F32)
            total = term if total is None else total + term
            start += size
        out[:, at] = (ratio[...] * total).astype(BF16)


def local_kernel(adj_t, dtotal, out):
    batches, nodes, _ = adj_t.shape
    for batch in range(batches):
        here = slice(batch * nodes, (batch + 1) * nodes)
        for at in tiles(dtotal.shape[1]):
            out[here, at] = jnp.dot(adj_t[batch], dtotal[here, at], preferred_element_type=F32)


def input_kernel(place, send_row, own, other, weight_own, weight_other, *refs):
    pieces, (out, result, sems) = refs[:-3], refs[-3:]
    rows, half = own.shape
    hot = hot_rows(send_row[...], rows).astype(BF16)
    grad = stack([piece.at[:, : 2 * half] for piece in pieces])
    me = place[0]
    copies = []
    for partial, weight, spot in ((own, weight_own, me), (other, weight_other, 1 - me)):
        for at in tiles(half):
            here = pl.ds(pl.multiple_of(spot * half + at.start, 512), at.stop - at.start)
            returned = lax.dot_general(grad, weight[at], NT, preferred_element_type=F32).astype(BF16)
            total = partial[:, at] + jnp.dot(hot, returned, preferred_element_type=F32)
            i = len(copies)
            result[i] = total.astype(BF16)
            copies.append(pltpu.make_async_copy(result.at[i], out.at[:, here], sems.at[i]))
            copies[-1].start()
    for copy in copies:
        copy.wait()


def bias_kernel(*refs):
    out = refs[-1]
    width = refs[0].shape[1] - out.shape[1]
    out[...] = sum(jnp.sum(piece[:, width:].astype(F32), axis=0, keepdims=True) for piece in refs[:-1])


def halve_kernel(*refs):
    pairs, (stay, leave) = refs[:-2], refs[-2:]
    half = stay.shape[0]
    for out, low in ((leave, half), (stay, 0)):
        here = slice(low, low + half)
        start = 0
        for keep, arrived in zip(pairs[::2], pairs[1::2]):
            at = slice(start, start + keep.shape[1])
            out[:, at] = (keep[here].astype(F32) + arrived[here].astype(F32)).astype(BF16)
            start = at.stop


def last_kernel(place, bias_mine, bias_theirs, *refs):
    out, bias_out = refs[-2:]
    start = 0
    for keep, arrived in zip(refs[:-2:2], refs[1:-2:2]):
        size = keep.shape[1]
        out[:, start : start + size] = keep[...].astype(F32) + arrived[...].astype(F32)
        start += size
    bias = bias_mine[...] + bias_theirs[...]
    count = bias_out.shape[1]
    bias_out[...] = jnp.where(place[0] == 0, bias[:, :count], bias[:, count : 2 * count])


def partners(parts, axis):
    turned = {0: 1, 1: 0}.get(axis, axis) if parts > 2 else axis
    return [(p * 2 + c, (p ^ (1 << (axis, turned)[c])) * 2 + c) for p in range(parts) for c in range(2)]


class Reduction:
    def __init__(self, order, parts, axes, keep, leave):
        self.order = order
        self.parts = parts
        self.axes = list(axes)
        self.send(keep, leave)

    def send(self, keep, leave):
        self.pairs = [(keep, lax.ppermute(leave, AXES, partners(self.parts, self.axes.pop(0))))]

    def join(self, other):
        self.pairs = other.pairs + self.pairs
        other.pairs = []

    def flat(self):
        return [x for pair in self.pairs for x in pair]

    def step(self):
        rows = self.pairs[0][0].shape[0]
        half = sds((rows // 2, sum(keep.shape[1] for keep, _ in self.pairs)), BF16)
        self.send(*self.order.run(halve_kernel, "halve", (half, half), self.flat()))


class Exchange:
    def __init__(self, order, parts, axes, size, pieces):
        self.order, self.parts, self.axes, self.size = order, parts, list(axes), size
        self.lists = halves(range(parts), self.axes[0])
        self.stay, leave = pieces
        self.arrived = lax.ppermute(leave, AXES, partners(parts, self.axes.pop(0)))

    def step(self):
        if not self.axes:
            return
        found = {r: (i, spot) for i in range(2) for spot, r in enumerate(self.lists[i])}
        axis = self.axes.pop(0)
        self.lists = halves(self.lists[0] + self.lists[1], axis)
        orders = [[found[r] for r in part] for part in self.lists]
        shape = sds(self.stay.shape, BF16)
        self.stay, leave = self.order.run(
            functools.partial(regroup_kernel, self.size, orders), "regroup", (shape, shape), (self.stay, self.arrived)
        )
        self.arrived = lax.ppermute(leave, AXES, partners(self.parts, axis))


def halves(distances, axis):
    return [[r for r in distances if (r >> axis) & 1 == side] for side in range(2)]


def local(parts, features, weight, bias, local_adj, send_index, recv_target, cotangent):
    batches, nodes, width = features.shape
    rows = batches * nodes
    half = width // 2
    core = lax.axis_index("mp").astype(jnp.int32)
    part = lax.axis_index("parts").astype(jnp.int32)
    place = jnp.stack([core, part])
    paired = parts & (parts - 1) == 0 and width % (2 * parts) == 0 and (width // (2 * parts)) % 16 == 0
    block = width // (2 * parts)

    feats = features.reshape(rows, width)
    cot = cotangent.reshape(rows, width)
    digits = parts.bit_length() - 1
    near = min(4, parts)
    far = parts // near
    orders = [None] * 4
    early = late = None
    if paired:
        late = list(range(digits))
        early = late[2:] + late[:2]
        back = [axis for axis in BACK if axis < digits] + list(range(len(BACK), digits))
        first, last = halves(range(parts), back[0]), list(range(parts))
        for axis in back:
            last = sum(halves(last, axis), [])
        across = [k * near + j for j in range(near) for k in range(far)]
        orders = [list(range(parts)), across, sum(first, []), last]
        if DIRECT:
            orders[2:] = [list(range(parts)), across]
            first = [[k * near + j for j in range(near)] for k in range(far)]
    slots = send_index.size
    per_part = slots // parts

    def move(pieces, stride):
        moved = list(pieces)
        for i in reversed(range(1, len(pieces))):
            perm = [(p, p ^ (i * stride)) for p in range(parts)]
            moved[i] = lax.ppermute(pieces[i], "parts", perm)
        return moved

    def exchange(values):
        moved = lax.all_to_all(
            values.reshape(parts, per_part, values.shape[1]), "parts", split_axis=0, concat_axis=0, tiled=True
        )
        return moved.reshape(values.shape)

    other = lax.ppermute(weight, "mp", SWAP)
    bias_own = bias.reshape(1, half)
    bias_other = lax.ppermute(bias_own, "mp", SWAP)
    order = Order(12 if paired else 48)
    run = order.run
    turn = (0, 1, 3, 2)
    pieces = far if paired else 1
    turned = jnp.transpose(send_index, turn), jnp.transpose(recv_target, turn)
    indices = [pltpu.VMEM(x.shape, jnp.int32) for x in turned]
    feats, *outgoing = run(
        functools.partial(outgoing_kernel, nodes, orders[0]),
        "outgoing",
        (sds((rows, width), BF16),) + (sds((slots // pieces, width), BF16),) * pieces,
        (),
        scalars=(place,),
        far=(feats, turned[0]),
        scratch=[indices[0], pltpu.SemaphoreType.DMA((5,))],
    )
    if paired:
        outgoing = move(outgoing, near)

    row = sds((1, slots), jnp.int32)
    mixed, mixed_t, ratio, ratio_row, adj_t, weight, send_row, recv_row, back_row = run(
        functools.partial(mix_kernel, orders),
        "mix",
        (
            sds((2, rows, half), BF16),
            sds((width, rows), BF16),
            sds((rows, 1), F32),
            sds((8, rows), F32),
            sds((batches, nodes, nodes), BF16),
            sds(weight.shape, BF16),
            row,
            row,
            row,
        ),
        (feats,),
        scalars=(place,),
        far=(weight, local_adj, *turned),
        scratch=[pltpu.VMEM(local_adj.shape, jnp.int32), *indices, pltpu.SemaphoreType.DMA((4,))],
    )
    pre, other = run(
        pre_own_kernel,
        "pre_own",
        (sds((rows, width), F32), sds(other.shape, BF16)),
        (mixed, weight),
        scalars=(place,),
        far=(other,),
        scratch=[pltpu.SemaphoreType.DMA(())],
    )
    if paired:
        arrived = run(
            functools.partial(
                regroup_kernel, per_part, [[(k, j) for k in range(far)] for j in range(near)]
            ),
            "regroup",
            (sds((far * per_part, width), BF16),) * near,
            outgoing,
        )
        arrived = move(arrived, 1)
    else:
        arrived = [exchange(outgoing[0])]
    (pre,) = run(
        pre_other_kernel,
        "pre_other",
        (sds((rows, width), F32),),
        (pre, mixed, other),
        scalars=(place,),
    )
    remote, bias_full = run(
        remote_kernel,
        "remote_product",
        (sds((2 * slots, width), BF16), sds((1, width), F32)),
        (weight, other, bias_own, bias_other, *arrived),
        scalars=(place,),
    )

    starts = [sum(CHUNKS[:i]) for i in range(len(CHUNKS))]
    act = None
    dpres, dpres_other, bias_terms, sums, dtotals, partials = [], [], [], [], [], []

    def gelu(i):
        nonlocal act
        size = CHUNKS[i]
        act, dpre, bias_term = run(
            functools.partial(gelu_kernel, starts[i]),
            "gelu",
            (sds((rows, width), BF16), sds((rows, size), BF16), sds((1, size), F32)),
            (recv_row, ratio, remote, pre, bias_full, cot),
            scratch=[pltpu.VMEM((rows, size), F32), pltpu.VMEM((rows, size), BF16), pltpu.SemaphoreType.DMA((3,))],
            keep=act,
        )
        dpres.append(dpre)
        dpres_other.append(lax.ppermute(dpre, "mp", SWAP))
        bias_terms.append(bias_term)

    def grad(i, mine, theirs):
        size = CHUNKS[i]
        shape = sds((half // 2, size), BF16)
        if paired:
            axes = early if i == FAR_FIRST else late
            spots = [sum(((r >> axes[::-1].index(axis)) & 1) << d for d, axis in enumerate(late[::-1])) for r in range(parts)]
            size_of = block
        else:
            spots, size_of = list(range(half // 128)), 128
        keep, leave = run(
            functools.partial(grad_kernel, spots, size_of),
            "grad",
            (shape, shape),
            (mine, theirs, dpres[i], dpres_other[i]),
        )
        if paired:
            sums.append(Reduction(order, parts, axes, keep, leave))
            return
        both = jnp.concatenate([keep, leave]).astype(F32)
        sums.append(lax.psum_scatter(both, "parts", scatter_dimension=0, tiled=True))

    extra = max(128, width // parts)
    pieces = (far if DIRECT else 2) if paired else 1
    for step, cost in zip(PLAN, COSTS):
        kind, number = step[0], int(step[1:] or 0)
        order.cost = cost
        if kind == "g":
            gelu(number)
        elif kind == "f":
            mine, theirs = run(
                functools.partial(finish_kernel, late, block),
                "finish_mixed",
                (sds((half, rows), BF16), sds((half, rows), BF16)),
                (recv_row, ratio_row, mixed_t, *arrived),
                scalars=(place,),
            )
            theirs = lax.ppermute(theirs, "mp", SWAP)
        elif kind == "d":
            grad(number, mine, theirs)
        elif kind == "s":
            sent = run(
                functools.partial(
                    sent_kernel, len(CHUNKS), parts, per_part, first if paired else [list(range(parts))]
                ),
                "sent_grads",
                (sds((slots // pieces, width + extra), BF16),) * pieces,
                (back_row, ratio_row, *dpres, *bias_terms),
                scalars=(place,),
                scratch=[pltpu.VMEM((8, width), F32)],
            )
            if paired:
                swap = move(sent, near) if DIRECT else Exchange(order, parts, back, per_part, sent)
            else:
                returned = [exchange(sent[0])]
        elif kind == "b":
            (dtotal,) = run(
                functools.partial(back_kernel, len(CHUNKS)),
                "back",
                (sds((rows, half), BF16),),
                (ratio, (weight, other)[number], *dpres),
            )
            dtotals.append(dtotal)
        elif kind == "l":
            (partial,) = run(local_kernel, "input_local", (sds((rows, half), F32),), (adj_t, dtotals[number]))
            partials.append(partial)
        elif kind == "i":
            if paired:
                returned = swap if DIRECT else [swap.stay, swap.arrived]
            (bias_mine,) = run(bias_kernel, "bias_sum", (sds((1, extra), F32),), returned)
            bias_theirs = lax.ppermute(bias_mine, "mp", SWAP)
            size = min(512, half)
            (input_grad,) = run(
                input_kernel,
                "input_gradient",
                (sds((rows, width), BF16),),
                (send_row, *partials, weight, other, *returned),
                scalars=(place,),
                scratch=[pltpu.VMEM((width // size, rows, size), BF16), pltpu.SemaphoreType.DMA((width // size,))],
                keep=None,
            )
        elif paired and kind == "r":
            if JOIN and number == 1 and len(sums[1].axes) == digits - 2:
                sums[1].join(sums[0])
            sums[number].step()
        elif paired and kind == "e":
            if DIRECT:
                swap = move(
                    run(
                        functools.partial(regroup_kernel, per_part, [[(k, j) for k in range(far)] for j in range(near)]),
                        "regroup",
                        (sds((far * per_part, width + extra), BF16),) * near,
                        swap,
                    ),
                    1,
                )
            else:
                swap.step()
    count = width // (2 * parts)
    if paired:
        weight_grad, bias_grad = run(
            last_kernel,
            "last_sum",
            (sds((block, width), F32), sds((1, count), F32)),
            [bias_mine, bias_theirs] + sum((s.flat() for s in sums), []),
            scalars=(place,),
        )
        bias_grad = bias_grad.reshape(count)
    else:
        weight_grad = jnp.concatenate(sums, axis=1)
        bias_all = (bias_mine + bias_theirs)[0]
        bias_grad = jnp.where(core == 0, bias_all[:count], bias_all[count : 2 * count])
    return (
        act.reshape(batches, nodes, width),
        input_grad.reshape(batches, nodes, width),
        weight_grad,
        bias_grad,
    )


def solution(mesh):
    return jax.shard_map(
        functools.partial(local, mesh.shape["parts"]),
        mesh=mesh,
        in_specs=(
            P("mp", "parts", None),
            P("mp", None),
            P("mp"),
            P("mp", "parts", None),
            P("mp", "parts", None, None),
            P("mp", "parts", None, None),
            P("mp", "parts", None),
        ),
        out_specs=(
            P("mp", "parts", None),
            P("mp", "parts", None),
            P(("parts", "mp"), None),
            P(("parts", "mp")),
        ),
        check_vma=False,
    )
```

```python
import functools
import math

import jax
import jax.numpy as jnp
from jax import lax
from jax.experimental import pallas as pl
from jax.experimental.pallas import tpu as pltpu
from jax.sharding import PartitionSpec as P

F32 = jnp.float32
BF16 = jnp.bfloat16
AXES = ("parts", "mp")
SWAP = ((0, 1), (1, 0))
GELU_C = math.sqrt(2.0 / math.pi)
GELU_A = 0.044715
CHUNKS = (1024, 768, 256)
FAR_FIRST = 2
BACK = (3, 2, 0, 1)
DIRECT = True
JOIN = False
PLAN = ('f', 'g0', 'g1', 'g2', 's', 'd0', 'd1', 'd2', 'e', 'r0', 'b0', 'r2', 'r1', 'r0', 'b1', 'l0', 'r1', 'r2', 'r0', 'r2', 'r1', 'l1', 'i')
COSTS = (1, 1000000000, 4000000000, 1, 8000000000, 16000000000, 1, 1, 4000000000, 1, 1, 4000000000, 2000000000, 4000000000, 1000000000, 1, 1, 1000000000, 1, 1, 1, 1, 1)
VMEM = pl.BlockSpec(memory_space=pltpu.VMEM)
SMEM = pl.BlockSpec(memory_space=pltpu.SMEM)
ANY = pl.BlockSpec(memory_space=pl.ANY)
HBM = pl.BlockSpec(memory_space=pltpu.HBM)
NT = (((1,), (1,)), ((), ()))


def sds(shape, dtype):
    return jax.ShapeDtypeStruct(shape, dtype)


class Order:
    def __init__(self, limit):
        self.token = None
        self.limit = limit
        self.cost = 1

    def run(self, kernel, name, out_shape, args, scalars=(), far=(), scratch=(), keep=False):
        specs = [SMEM] * len(scalars) + [HBM] * len(far) + [VMEM] * len(args)
        args = [*scalars, *(pltpu.with_memory_space_constraint(x, pltpu.HBM) for x in far), *args]
        used = len(args)
        aliases = {}
        if keep is not None and keep is not False:
            aliases = {len(args): 0}
            args.append(keep)
            specs.append(ANY)
        if self.token is not None:
            args.append(self.token)
            specs.append(VMEM)
        count, results = len(args), len(out_shape)

        def body(*refs):
            refs[count + results][...] = jnp.zeros((8, 128), F32)
            kernel(*refs[:used], *refs[count : count + results], *refs[count + results + 1 :])

        *out, self.token = pl.pallas_call(
            body,
            name=name,
            in_specs=specs,
            out_specs=((VMEM if keep is False else ANY,) + (VMEM,) * results),
            out_shape=(*out_shape, sds((8, 128), F32)),
            scratch_shapes=scratch,
            input_output_aliases=aliases,
            compiler_params=pltpu.CompilerParams(vmem_limit_bytes=self.limit * 2**20),
            cost_estimate=pl.CostEstimate(flops=self.cost, bytes_accessed=1, transcendentals=0),
        )(*args)
        return out


def hot_rows(index_row, rows):
    match = lax.broadcasted_iota(jnp.int32, (rows, index_row.shape[1]), 0) == index_row
    return jnp.where(match, 1.0, 0.0)


def tiles(width, size=512):
    return [slice(i, min(i + size, width)) for i in range(0, width, size)]


def index_column(index, part, nodes, order=None, turned=0):
    batches, _, depth, parts = index.shape
    slots = batches * parts * depth
    slot = lax.broadcasted_iota(jnp.int32, (slots, parts), 0)
    spot, rest = lax.div(slot, batches * depth), lax.rem(slot, batches * depth)
    if order is not None:
        apart = jnp.zeros((slots, parts), jnp.int32)
        for i, distance in enumerate(order):
            apart = jnp.where(spot == i, distance, apart)
        spot = turn_digits(apart, turned) ^ part
    here = lax.broadcasted_iota(jnp.int32, (slots, parts), 1) == spot
    total = jnp.zeros((slots, parts), jnp.int32)
    for batch in range(batches):
        node = index[batch, 0]
        node = jnp.where(node < 0, -1, node + batch * nodes)
        for h in range(depth):
            total = jnp.where(rest == batch * depth + h, node[h : h + 1], total)
    return jnp.sum(jnp.where(here, total, 0), axis=1, keepdims=True)


def turn_digits(value, turned):
    differ = (value ^ lax.shift_right_logical(value, 1)) & turned
    return value ^ differ ^ (differ << 1)


def as_row(column):
    return jnp.broadcast_to(column, (column.shape[0], 128)).T[:1]


def hot_cols(index_col, cols):
    match = lax.broadcasted_iota(jnp.int32, (index_col.shape[0], cols), 1) == index_col
    return jnp.where(match, 1.0, 0.0)


def outgoing_kernel(nodes, order, place, feats, send_far, here, *rest):
    outs, (send, sems) = rest[:-2], rest[-2:]
    width = feats.shape[1]
    ranges = tiles(width, width // (sems.shape[0] - 1))
    copies = [pltpu.make_async_copy(feats.at[:, at], here.at[:, at], sems.at[i]) for i, at in enumerate(ranges)]
    fetch = pltpu.make_async_copy(send_far, send, sems.at[len(ranges)])
    for copy in (fetch, *copies):
        copy.start()
    fetch.wait()
    hot = hot_cols(index_column(send, place[1], nodes, order), feats.shape[0]).astype(BF16)
    size = outs[0].shape[0]
    for at, copy in zip(ranges, copies):
        copy.wait()
        value = jnp.dot(hot, here[:, at], preferred_element_type=F32)
        for i, out in enumerate(outs):
            out[:, at] = value[i * size : (i + 1) * size].astype(BF16)


def regroup_kernel(size, orders, *refs):
    pieces, outs = refs[: -len(orders)], refs[-len(orders) :]
    values = [piece[...].astype(F32) for piece in pieces]
    for order, out in zip(orders, outs):
        blocks = [values[i][block * size : (block + 1) * size] for i, block in order]
        out[...] = jnp.concatenate(blocks, axis=0).astype(BF16)


def stack(pieces):
    return jnp.concatenate([piece[...] for piece in pieces], axis=0)


def mix_kernel(orders, place, weight, edges, send_far, recv_far, feats, *refs):
    mixed, mixed_t, ratio, ratio_row, adj_t, own, send_row, recv_row, back_row, adj, send, recv, sems = refs
    copies = [
        pltpu.make_async_copy(source, target, sems.at[i])
        for i, (source, target) in enumerate(((recv_far, recv), (send_far, send), (edges, adj), (weight, own)))
    ]
    for copy in copies:
        copy.start()
    for copy in copies[:3]:
        copy.wait()
    me, part = place[0], place[1]
    nodes = adj.shape[1]
    recv_row[...] = as_row(index_column(recv, part, nodes, orders[1]))
    back_row[...] = as_row(index_column(recv, part, nodes, orders[2], 0 if DIRECT else me))
    send_row[...] = as_row(index_column(send, part, nodes, orders[3], 0 if DIRECT else me))
    batches, nodes, _ = adj.shape
    half = mixed.shape[2]
    eye = lax.broadcasted_iota(jnp.int32, (nodes, nodes), 0) == lax.broadcasted_iota(
        jnp.int32, (nodes, nodes), 1
    )
    for batch in range(batches):
        here = slice(batch * nodes, (batch + 1) * nodes)
        count = adj[batch].astype(F32)
        hot = hot_rows(recv_row[...] - batch * nodes, nodes)
        degree = jnp.sum(count, axis=1, keepdims=True) + jnp.sum(hot, axis=1, keepdims=True)
        scale = 1.0 / (1.0 + degree)
        ratio[here] = scale
        ratio_row[:, here] = jnp.broadcast_to(scale, (nodes, 128)).T[:8]
        count = count + jnp.where(eye, 2.0, 0.0)
        adj_t[batch] = count.T.astype(BF16)
        count = count.astype(BF16)
        for at in tiles(feats.shape[1]):
            value = scale * jnp.dot(count, feats[here, at], preferred_element_type=F32)
            low = at.start % half
            mixed[at.start // half, here, low : low + at.stop - at.start] = value.astype(BF16)
            mixed_t[at, here] = value.T.astype(BF16)
    copies[3].wait()


def pre_own_kernel(place, mixed, weight, pre):
    me = place[0]
    for at in tiles(pre.shape[1]):
        pre[:, at] = jnp.dot(mixed[me], weight[:, at], preferred_element_type=F32)


def pre_other_kernel(place, before, mixed, weight, pre):
    me = place[0]
    for at in tiles(pre.shape[1]):
        pre[:, at] = before[:, at] + jnp.dot(mixed[1 - me], weight[:, at], preferred_element_type=F32)


def finish_kernel(axes, block, place, recv_row, ratio_row, mixed_t, *refs):
    pieces, (mine, theirs) = refs[:-2], refs[-2:]
    me, part = place[0], place[1]
    first = me == 0
    rows = mixed_t.shape[1]
    hot = hot_rows(recv_row[...], rows).T.astype(BF16)
    scale = ratio_row[0:1]
    for at in tiles(mixed_t.shape[0], 256):
        remote = jnp.dot(stack([piece.at[:, at] for piece in pieces]).T, hot, preferred_element_type=F32)
        value = (mixed_t[at].astype(F32) + scale * remote).reshape(128 // block, 2, block, rows)
        for out, swap in ((mine, False), (theirs, True)):
            low, high = (1, 0) if swap else (0, 1)
            chosen = jnp.where(first, value[:, low], value[:, high])
            if axes is None:
                out[at.start // 2 : at.stop // 2] = chosen.reshape(128, rows).astype(BF16)
                continue
            owner = 1 - me if swap else me
            for i in range(128 // block):
                spot = spot_of(axes, part, owner, at.start // (2 * block) + i)
                out[pl.ds(pl.multiple_of(spot * block, block), block)] = chosen[i].astype(BF16)


def remote_kernel(place, own, other, bias_own, bias_other, *refs):
    pieces, (out, bias) = refs[:-2], refs[-2:]
    half = own.shape[0]
    me = place[0]
    spots = out.shape[0] // 2
    here = stack([piece.at[:, pl.ds(pl.multiple_of(me * half, half), half)] for piece in pieces])
    there = stack([piece.at[:, pl.ds(pl.multiple_of((1 - me) * half, half), half)] for piece in pieces])
    for at in tiles(own.shape[1]):
        product = jnp.dot(here, own[:, at], preferred_element_type=F32)
        product += jnp.dot(there, other[:, at], preferred_element_type=F32)
        high = product.astype(BF16)
        out[:spots, at] = high
        out[spots:, at] = (product - high.astype(F32)).astype(BF16)
    mine, theirs = bias_own[...].astype(F32), bias_other[...].astype(F32)
    bias[:, :half] = jnp.where(me == 0, mine, theirs)
    bias[:, half:] = jnp.where(me == 0, theirs, mine)


def gelu_kernel(start, recv_row, ratio, remote, pre, bias, cot, act, dpre, bias_term, value, result, sems):
    rows, size = dpre.shape
    at = slice(start, start + size)
    hot = hot_rows(recv_row[...], rows).astype(BF16)
    value[...] = pre[:, at] + bias[:, at] + ratio[...] * jnp.dot(
        jnp.concatenate([hot, hot], axis=1), remote[:, at], preferred_element_type=F32
    )
    step = 64

    def body(i, total):
        here = pl.ds(pl.multiple_of(i * step, step), step)
        v = value[here]
        square = v * v
        left = 0.5 + 0.5 * jnp.tanh(v * (GELU_C + GELU_C * GELU_A * square))
        out = v * left
        result[here] = out.astype(BF16)
        slope = left + (out - out * left) * (2.0 * GELU_C + 6.0 * GELU_C * GELU_A * square)
        grad = (cot[here, at].astype(F32) * slope).astype(BF16)
        dpre[here] = grad
        return total + grad.astype(F32).reshape(step // 8, 8, size).sum(axis=0)

    total = jnp.zeros((8, size), F32)
    pieces = sems.shape[0]
    steps = rows // step
    copies = []
    for piece in range(pieces):
        low, high = piece * steps // pieces, (piece + 1) * steps // pieces
        total = lax.fori_loop(low, high, body, total)
        here = slice(low * step, high * step)
        copies.append(pltpu.make_async_copy(result.at[here], act.at[here, at], sems.at[piece]))
        copies[-1].start()
    bias_term[...] = jnp.sum(total, axis=0, keepdims=True)
    for copy in copies:
        copy.wait()


def spot_of(axes, part, owner, index):
    apart = turn_digits(part ^ index, owner)
    spot = 0
    for axis in axes:
        spot = spot * 2 + (lax.shift_right_logical(apart, axis) & 1)
    return spot


def grad_kernel(order, block, mine, theirs, dpre_mine, dpre_theirs, keep, leave):
    half = keep.shape[0]
    count = min(256 // block, len(order) // 2)
    for i in range(0, len(order), count):
        spots = [slice(spot * block, (spot + 1) * block) for spot in order[i : i + count]]
        total = jnp.dot(stack([mine.at[at] for at in spots]), dpre_mine[...], preferred_element_type=F32)
        total += jnp.dot(stack([theirs.at[at] for at in spots]), dpre_theirs[...], preferred_element_type=F32)
        low = i * block % half
        out = keep if i * block < half else leave
        out[low : low + count * block] = total.astype(BF16)


def sent_kernel(chunks, parts, per_part, sources, place, recv_row, ratio_row, *refs):
    dpres, bias_terms, outs = refs[:chunks], refs[chunks : 2 * chunks], refs[2 * chunks : -1]
    lines = refs[-1]
    width = lines.shape[1]
    rows = ratio_row.shape[1]
    hot = (hot_rows(recv_row[...], rows).T * ratio_row[0:1]).astype(BF16)
    me, part = place[0], place[1]
    size = outs[0].shape[0]
    start = 0
    for dpre in dpres:
        at = slice(start, start + dpre.shape[1])
        value = jnp.dot(hot, dpre[...], preferred_element_type=F32)
        for i, out in enumerate(outs):
            out[:, at] = value[i * size : (i + 1) * size].astype(BF16)
        start = at.stop
    bias = jnp.concatenate([term[...] for term in bias_terms], axis=1)
    high = bias.astype(BF16).astype(F32)
    middle = (bias - high).astype(BF16).astype(F32)
    line = lax.broadcasted_iota(jnp.int32, (8, width), 0)
    lines[...] = jnp.where(line == 0, high, jnp.where(line == 1, middle, bias - high - middle))
    count = width // parts
    line = lax.broadcasted_iota(jnp.int32, (8, count), 0)
    for i, out in enumerate(outs):
        pieces = []
        for source in sources[i]:
            if len(outs) > 1:
                to = part ^ turn_digits(source, 0 if DIRECT else me)
                piece = lines[:, pl.ds(pl.multiple_of(to * count, count), count)]
            else:
                piece = lines[:, source * count : (source + 1) * count]
            piece = jnp.where(line < 3, piece, 0.0)
            if count < 128:
                piece = jnp.concatenate([piece, jnp.zeros((8, 128 - count), F32)], axis=1)
            if per_part > 8:
                piece = jnp.concatenate([piece, jnp.zeros((per_part - 8, piece.shape[1]), F32)], axis=0)
            pieces.append(piece)
        out[:, width:] = jnp.concatenate(pieces, axis=0).astype(BF16)


def back_kernel(chunks, ratio, weight, *refs):
    dpres, out = refs[:chunks], refs[chunks]
    for at in tiles(weight.shape[0], 256):
        total = None
        start = 0
        for dpre in dpres:
            size = dpre.shape[1]
            term = lax.dot_general(dpre[...], weight[at, start : start + size], NT, preferred_element_type=F32)
            total = term if total is None else total + term
            start += size
        out[:, at] = (ratio[...] * total).astype(BF16)


def local_kernel(adj_t, dtotal, out):
    batches, nodes, _ = adj_t.shape
    for batch in range(batches):
        here = slice(batch * nodes, (batch + 1) * nodes)
        for at in tiles(dtotal.shape[1]):
            out[here, at] = jnp.dot(adj_t[batch], dtotal[here, at], preferred_element_type=F32)


def input_kernel(place, send_row, own, other, weight_own, weight_other, *refs):
    pieces, (out, result, sems) = refs[:-3], refs[-3:]
    rows, half = own.shape
    hot = hot_rows(send_row[...], rows).astype(BF16)
    grad = stack([piece.at[:, : 2 * half] for piece in pieces])
    me = place[0]
    copies = []
    for partial, weight, spot in ((own, weight_own, me), (other, weight_other, 1 - me)):
        for at in tiles(half):
            here = pl.ds(pl.multiple_of(spot * half + at.start, 512), at.stop - at.start)
            returned = lax.dot_general(grad, weight[at], NT, preferred_element_type=F32).astype(BF16)
            total = partial[:, at] + jnp.dot(hot, returned, preferred_element_type=F32)
            i = len(copies)
            result[i] = total.astype(BF16)
            copies.append(pltpu.make_async_copy(result.at[i], out.at[:, here], sems.at[i]))
            copies[-1].start()
    for copy in copies:
        copy.wait()


def bias_kernel(*refs):
    out = refs[-1]
    width = refs[0].shape[1] - out.shape[1]
    out[...] = sum(jnp.sum(piece[:, width:].astype(F32), axis=0, keepdims=True) for piece in refs[:-1])


def halve_kernel(*refs):
    pairs, (stay, leave) = refs[:-2], refs[-2:]
    half = stay.shape[0]
    for out, low in ((leave, half), (stay, 0)):
        here = slice(low, low + half)
        start = 0
        for keep, arrived in zip(pairs[::2], pairs[1::2]):
            at = slice(start, start + keep.shape[1])
            out[:, at] = (keep[here].astype(F32) + arrived[here].astype(F32)).astype(BF16)
            start = at.stop


def last_kernel(place, bias_mine, bias_theirs, *refs):
    out, bias_out = refs[-2:]
    start = 0
    for keep, arrived in zip(refs[:-2:2], refs[1:-2:2]):
        size = keep.shape[1]
        out[:, start : start + size] = keep[...].astype(F32) + arrived[...].astype(F32)
        start += size
    bias = bias_mine[...] + bias_theirs[...]
    count = bias_out.shape[1]
    bias_out[...] = jnp.where(place[0] == 0, bias[:, :count], bias[:, count : 2 * count])


def partners(parts, axis):
    turned = {0: 1, 1: 0}.get(axis, axis) if parts > 2 else axis
    return [(p * 2 + c, (p ^ (1 << (axis, turned)[c])) * 2 + c) for p in range(parts) for c in range(2)]


class Reduction:
    def __init__(self, order, parts, axes, keep, leave):
        self.order = order
        self.parts = parts
        self.axes = list(axes)
        self.send(keep, leave)

    def send(self, keep, leave):
        self.pairs = [(keep, lax.ppermute(leave, AXES, partners(self.parts, self.axes.pop(0))))]

    def join(self, other):
        self.pairs = other.pairs + self.pairs
        other.pairs = []

    def flat(self):
        return [x for pair in self.pairs for x in pair]

    def step(self):
        rows = self.pairs[0][0].shape[0]
        half = sds((rows // 2, sum(keep.shape[1] for keep, _ in self.pairs)), BF16)
        self.send(*self.order.run(halve_kernel, "halve", (half, half), self.flat()))


class Exchange:
    def __init__(self, order, parts, axes, size, pieces):
        self.order, self.parts, self.axes, self.size = order, parts, list(axes), size
        self.lists = halves(range(parts), self.axes[0])
        self.stay, leave = pieces
        self.arrived = lax.ppermute(leave, AXES, partners(parts, self.axes.pop(0)))

    def step(self):
        if not self.axes:
            return
        found = {r: (i, spot) for i in range(2) for spot, r in enumerate(self.lists[i])}
        axis = self.axes.pop(0)
        self.lists = halves(self.lists[0] + self.lists[1], axis)
        orders = [[found[r] for r in part] for part in self.lists]
        shape = sds(self.stay.shape, BF16)
        self.stay, leave = self.order.run(
            functools.partial(regroup_kernel, self.size, orders), "regroup", (shape, shape), (self.stay, self.arrived)
        )
        self.arrived = lax.ppermute(leave, AXES, partners(self.parts, axis))


def halves(distances, axis):
    return [[r for r in distances if (r >> axis) & 1 == side] for side in range(2)]


def local(parts, features, weight, bias, local_adj, send_index, recv_target, cotangent):
    batches, nodes, width = features.shape
    rows = batches * nodes
    half = width // 2
    core = lax.axis_index("mp").astype(jnp.int32)
    part = lax.axis_index("parts").astype(jnp.int32)
    place = jnp.stack([core, part])
    paired = parts & (parts - 1) == 0 and width % (2 * parts) == 0 and (width // (2 * parts)) % 16 == 0
    block = width // (2 * parts)

    feats = features.reshape(rows, width)
    cot = cotangent.reshape(rows, width)
    digits = parts.bit_length() - 1
    near = min(4, parts)
    far = parts // near
    orders = [None] * 4
    early = late = None
    if paired:
        late = list(range(digits))
        early = late[2:] + late[:2]
        back = [axis for axis in BACK if axis < digits] + list(range(len(BACK), digits))
        first, last = halves(range(parts), back[0]), list(range(parts))
        for axis in back:
            last = sum(halves(last, axis), [])
        across = [k * near + j for j in range(near) for k in range(far)]
        orders = [list(range(parts)), across, sum(first, []), last]
        if DIRECT:
            orders[2:] = [list(range(parts)), across]
            first = [[k * near + j for j in range(near)] for k in range(far)]
    slots = send_index.size
    per_part = slots // parts

    def move(pieces, stride):
        moved = list(pieces)
        for i in reversed(range(1, len(pieces))):
            perm = [(p, p ^ (i * stride)) for p in range(parts)]
            moved[i] = lax.ppermute(pieces[i], "parts", perm)
        return moved

    def exchange(values):
        moved = lax.all_to_all(
            values.reshape(parts, per_part, values.shape[1]), "parts", split_axis=0, concat_axis=0, tiled=True
        )
        return moved.reshape(values.shape)

    other = lax.ppermute(weight, "mp", SWAP)
    bias_own = bias.reshape(1, half)
    bias_other = lax.ppermute(bias_own, "mp", SWAP)
    order = Order(12 if paired else 48)
    run = order.run
    turn = (0, 1, 3, 2)
    pieces = far if paired else 1
    turned = jnp.transpose(send_index, turn), jnp.transpose(recv_target, turn)
    indices = [pltpu.VMEM(x.shape, jnp.int32) for x in turned]
    feats, *outgoing = run(
        functools.partial(outgoing_kernel, nodes, orders[0]),
        "outgoing",
        (sds((rows, width), BF16),) + (sds((slots // pieces, width), BF16),) * pieces,
        (),
        scalars=(place,),
        far=(feats, turned[0]),
        scratch=[indices[0], pltpu.SemaphoreType.DMA((5,))],
    )
    if paired:
        outgoing = move(outgoing, near)

    row = sds((1, slots), jnp.int32)
    order.cost = 6 * 10**10
    mixed, mixed_t, ratio, ratio_row, adj_t, weight, send_row, recv_row, back_row = run(
        functools.partial(mix_kernel, orders),
        "mix",
        (
            sds((2, rows, half), BF16),
            sds((width, rows), BF16),
            sds((rows, 1), F32),
            sds((8, rows), F32),
            sds((batches, nodes, nodes), BF16),
            sds(weight.shape, BF16),
            row,
            row,
            row,
        ),
        (feats,),
        scalars=(place,),
        far=(weight, local_adj, *turned),
        scratch=[pltpu.VMEM(local_adj.shape, jnp.int32), *indices, pltpu.SemaphoreType.DMA((4,))],
    )
    order.cost = 1
    (pre,) = run(pre_own_kernel, "pre_own", (sds((rows, width), F32),), (mixed, weight), scalars=(place,))
    if paired:
        arrived = run(
            functools.partial(
                regroup_kernel, per_part, [[(k, j) for k in range(far)] for j in range(near)]
            ),
            "regroup",
            (sds((far * per_part, width), BF16),) * near,
            outgoing,
        )
        arrived = move(arrived, 1)
    else:
        arrived = [exchange(outgoing[0])]
    (pre,) = run(
        pre_other_kernel, "pre_other", (sds((rows, width), F32),), (pre, mixed, other), scalars=(place,)
    )
    remote, bias_full = run(
        remote_kernel,
        "remote_product",
        (sds((2 * slots, width), BF16), sds((1, width), F32)),
        (weight, other, bias_own, bias_other, *arrived),
        scalars=(place,),
    )

    starts = [sum(CHUNKS[:i]) for i in range(len(CHUNKS))]
    act = None
    dpres, dpres_other, bias_terms, sums, dtotals, partials = [], [], [], [], [], []

    def gelu(i):
        nonlocal act
        size = CHUNKS[i]
        act, dpre, bias_term = run(
            functools.partial(gelu_kernel, starts[i]),
            "gelu",
            (sds((rows, width), BF16), sds((rows, size), BF16), sds((1, size), F32)),
            (recv_row, ratio, remote, pre, bias_full, cot),
            scratch=[pltpu.VMEM((rows, size), F32), pltpu.VMEM((rows, size), BF16), pltpu.SemaphoreType.DMA((3,))],
            keep=act,
        )
        dpres.append(dpre)
        dpres_other.append(lax.ppermute(dpre, "mp", SWAP))
        bias_terms.append(bias_term)

    def grad(i, mine, theirs):
        size = CHUNKS[i]
        shape = sds((half // 2, size), BF16)
        if paired:
            axes = early if i == FAR_FIRST else late
            spots = [sum(((r >> axes[::-1].index(axis)) & 1) << d for d, axis in enumerate(late[::-1])) for r in range(parts)]
            size_of = block
        else:
            spots, size_of = list(range(half // 128)), 128
        keep, leave = run(
            functools.partial(grad_kernel, spots, size_of),
            "grad",
            (shape, shape),
            (mine, theirs, dpres[i], dpres_other[i]),
        )
        if paired:
            sums.append(Reduction(order, parts, axes, keep, leave))
            return
        both = jnp.concatenate([keep, leave]).astype(F32)
        sums.append(lax.psum_scatter(both, "parts", scatter_dimension=0, tiled=True))

    extra = max(128, width // parts)
    pieces = (far if DIRECT else 2) if paired else 1
    for step, cost in zip(PLAN, COSTS):
        kind, number = step[0], int(step[1:] or 0)
        order.cost = cost
        if kind == "g":
            gelu(number)
        elif kind == "f":
            mine, theirs = run(
                functools.partial(finish_kernel, late, block),
                "finish_mixed",
                (sds((half, rows), BF16), sds((half, rows), BF16)),
                (recv_row, ratio_row, mixed_t, *arrived),
                scalars=(place,),
            )
            theirs = lax.ppermute(theirs, "mp", SWAP)
        elif kind == "d":
            grad(number, mine, theirs)
        elif kind == "s":
            sent = run(
                functools.partial(
                    sent_kernel, len(CHUNKS), parts, per_part, first if paired else [list(range(parts))]
                ),
                "sent_grads",
                (sds((slots // pieces, width + extra), BF16),) * pieces,
                (back_row, ratio_row, *dpres, *bias_terms),
                scalars=(place,),
                scratch=[pltpu.VMEM((8, width), F32)],
            )
            if paired:
                swap = move(sent, near) if DIRECT else Exchange(order, parts, back, per_part, sent)
            else:
                returned = [exchange(sent[0])]
        elif kind == "b":
            (dtotal,) = run(
                functools.partial(back_kernel, len(CHUNKS)),
                "back",
                (sds((rows, half), BF16),),
                (ratio, (weight, other)[number], *dpres),
            )
            dtotals.append(dtotal)
        elif kind == "l":
            (partial,) = run(local_kernel, "input_local", (sds((rows, half), F32),), (adj_t, dtotals[number]))
            partials.append(partial)
        elif kind == "i":
            if paired:
                returned = swap if DIRECT else [swap.stay, swap.arrived]
            (bias_mine,) = run(bias_kernel, "bias_sum", (sds((1, extra), F32),), returned)
            bias_theirs = lax.ppermute(bias_mine, "mp", SWAP)
            size = min(512, half)
            (input_grad,) = run(
                input_kernel,
                "input_gradient",
                (sds((rows, width), BF16),),
                (send_row, *partials, weight, other, *returned),
                scalars=(place,),
                scratch=[pltpu.VMEM((width // size, rows, size), BF16), pltpu.SemaphoreType.DMA((width // size,))],
                keep=None,
            )
        elif paired and kind == "r":
            if JOIN and number == 1 and len(sums[1].axes) == digits - 2:
                sums[1].join(sums[0])
            sums[number].step()
        elif paired and kind == "e":
            if DIRECT:
                swap = move(
                    run(
                        functools.partial(regroup_kernel, per_part, [[(k, j) for k in range(far)] for j in range(near)]),
                        "regroup",
                        (sds((far * per_part, width + extra), BF16),) * near,
                        swap,
                    ),
                    1,
                )
            else:
                swap.step()
    count = width // (2 * parts)
    if paired:
        weight_grad, bias_grad = run(
            last_kernel,
            "last_sum",
            (sds((block, width), F32), sds((1, count), F32)),
            [bias_mine, bias_theirs] + sum((s.flat() for s in sums), []),
            scalars=(place,),
        )
        bias_grad = bias_grad.reshape(count)
    else:
        weight_grad = jnp.concatenate(sums, axis=1)
        bias_all = (bias_mine + bias_theirs)[0]
        bias_grad = jnp.where(core == 0, bias_all[:count], bias_all[count : 2 * count])
    return (
        act.reshape(batches, nodes, width),
        input_grad.reshape(batches, nodes, width),
        weight_grad,
        bias_grad,
    )


def solution(mesh):
    return jax.shard_map(
        functools.partial(local, mesh.shape["parts"]),
        mesh=mesh,
        in_specs=(
            P("mp", "parts", None),
            P("mp", None),
            P("mp"),
            P("mp", "parts", None),
            P("mp", "parts", None, None),
            P("mp", "parts", None, None),
            P("mp", "parts", None),
        ),
        out_specs=(
            P("mp", "parts", None),
            P("mp", "parts", None),
            P(("parts", "mp"), None),
            P(("parts", "mp")),
        ),
        check_vma=False,
    )
```

```python
import functools
import math

import jax
import jax.numpy as jnp
from jax import lax
from jax.experimental import pallas as pl
from jax.experimental.pallas import tpu as pltpu
from jax.sharding import PartitionSpec as P

F32 = jnp.float32
BF16 = jnp.bfloat16
AXES = ("parts", "mp")
SWAP = ((0, 1), (1, 0))
GELU_C = math.sqrt(2.0 / math.pi)
GELU_A = 0.044715
CHUNKS = (1024, 768, 256)
FAR_FIRST = 2
BACK = (3, 2, 0, 1)
DIRECT = True
JOIN = False
PLAN = ('f', 'g0', 'g1', 'g2', 's', 'd0', 'd1', 'd2', 'e', 'r0', 'b0', 'r2', 'r1', 'r0', 'b1', 'l0', 'r1', 'r2', 'r0', 'r2', 'r1', 'l1', 'i')
COSTS = (1, 1000000000, 4000000000, 1, 8000000000, 16000000000, 1, 1, 4000000000, 1, 1, 4000000000, 2000000000, 4000000000, 1000000000, 1, 1, 1000000000, 1, 1, 1, 1, 1)
VMEM = pl.BlockSpec(memory_space=pltpu.VMEM)
SMEM = pl.BlockSpec(memory_space=pltpu.SMEM)
ANY = pl.BlockSpec(memory_space=pl.ANY)
HBM = pl.BlockSpec(memory_space=pltpu.HBM)
NT = (((1,), (1,)), ((), ()))


def sds(shape, dtype):
    return jax.ShapeDtypeStruct(shape, dtype)


class Order:
    def __init__(self, limit):
        self.token = None
        self.limit = limit
        self.cost = 1

    def run(self, kernel, name, out_shape, args, scalars=(), far=(), scratch=(), keep=False):
        specs = [SMEM] * len(scalars) + [HBM] * len(far) + [VMEM] * len(args)
        args = [*scalars, *(pltpu.with_memory_space_constraint(x, pltpu.HBM) for x in far), *args]
        used = len(args)
        aliases = {}
        if keep is not None and keep is not False:
            aliases = {len(args): 0}
            args.append(keep)
            specs.append(ANY)
        if self.token is not None:
            args.append(self.token)
            specs.append(VMEM)
        count, results = len(args), len(out_shape)

        def body(*refs):
            refs[count + results][...] = jnp.zeros((8, 128), F32)
            kernel(*refs[:used], *refs[count : count + results], *refs[count + results + 1 :])

        *out, self.token = pl.pallas_call(
            body,
            name=name,
            in_specs=specs,
            out_specs=((VMEM if keep is False else ANY,) + (VMEM,) * results),
            out_shape=(*out_shape, sds((8, 128), F32)),
            scratch_shapes=scratch,
            input_output_aliases=aliases,
            compiler_params=pltpu.CompilerParams(vmem_limit_bytes=self.limit * 2**20),
            cost_estimate=pl.CostEstimate(flops=self.cost, bytes_accessed=1, transcendentals=0),
        )(*args)
        return out


def hot_rows(index_row, rows):
    match = lax.broadcasted_iota(jnp.int32, (rows, index_row.shape[1]), 0) == index_row
    return jnp.where(match, 1.0, 0.0)


def tiles(width, size=512):
    return [slice(i, min(i + size, width)) for i in range(0, width, size)]


def index_column(index, part, nodes, order=None, turned=0):
    batches, _, depth, parts = index.shape
    slots = batches * parts * depth
    slot = lax.broadcasted_iota(jnp.int32, (slots, parts), 0)
    spot, rest = lax.div(slot, batches * depth), lax.rem(slot, batches * depth)
    if order is not None:
        apart = jnp.zeros((slots, parts), jnp.int32)
        for i, distance in enumerate(order):
            apart = jnp.where(spot == i, distance, apart)
        spot = turn_digits(apart, turned) ^ part
    here = lax.broadcasted_iota(jnp.int32, (slots, parts), 1) == spot
    total = jnp.zeros((slots, parts), jnp.int32)
    for batch in range(batches):
        node = index[batch, 0]
        node = jnp.where(node < 0, -1, node + batch * nodes)
        for h in range(depth):
            total = jnp.where(rest == batch * depth + h, node[h : h + 1], total)
    return jnp.sum(jnp.where(here, total, 0), axis=1, keepdims=True)


def turn_digits(value, turned):
    differ = (value ^ lax.shift_right_logical(value, 1)) & turned
    return value ^ differ ^ (differ << 1)


def as_row(column):
    return jnp.broadcast_to(column, (column.shape[0], 128)).T[:1]


def hot_cols(index_col, cols):
    match = lax.broadcasted_iota(jnp.int32, (index_col.shape[0], cols), 1) == index_col
    return jnp.where(match, 1.0, 0.0)


def outgoing_kernel(nodes, order, place, feats, send_far, here, *rest):
    outs, (send, sems) = rest[:-2], rest[-2:]
    width = feats.shape[1]
    ranges = tiles(width, width // (sems.shape[0] - 1))
    copies = [pltpu.make_async_copy(feats.at[:, at], here.at[:, at], sems.at[i]) for i, at in enumerate(ranges)]
    fetch = pltpu.make_async_copy(send_far, send, sems.at[len(ranges)])
    for copy in (fetch, *copies):
        copy.start()
    fetch.wait()
    hot = hot_cols(index_column(send, place[1], nodes, order), feats.shape[0]).astype(BF16)
    size = outs[0].shape[0]
    for at, copy in zip(ranges, copies):
        copy.wait()
        value = jnp.dot(hot, here[:, at], preferred_element_type=F32)
        for i, out in enumerate(outs):
            out[:, at] = value[i * size : (i + 1) * size].astype(BF16)


def regroup_kernel(size, orders, *refs):
    pieces, outs = refs[: -len(orders)], refs[-len(orders) :]
    values = [piece[...].astype(F32) for piece in pieces]
    for order, out in zip(orders, outs):
        blocks = [values[i][block * size : (block + 1) * size] for i, block in order]
        out[...] = jnp.concatenate(blocks, axis=0).astype(BF16)


def stack(pieces):
    return jnp.concatenate([piece[...] for piece in pieces], axis=0)


def mix_kernel(orders, place, weight, edges, send_far, recv_far, feats, *refs):
    mixed, mixed_t, ratio, ratio_row, adj_t, own, send_row, recv_row, back_row, adj, send, recv, sems = refs
    copies = [
        pltpu.make_async_copy(source, target, sems.at[i])
        for i, (source, target) in enumerate(((recv_far, recv), (send_far, send), (edges, adj), (weight, own)))
    ]
    for copy in copies:
        copy.start()
    for copy in copies[:3]:
        copy.wait()
    me, part = place[0], place[1]
    nodes = adj.shape[1]
    recv_row[...] = as_row(index_column(recv, part, nodes, orders[1]))
    back_row[...] = as_row(index_column(recv, part, nodes, orders[2], 0 if DIRECT else me))
    send_row[...] = as_row(index_column(send, part, nodes, orders[3], 0 if DIRECT else me))
    batches, nodes, _ = adj.shape
    half = mixed.shape[2]
    eye = lax.broadcasted_iota(jnp.int32, (nodes, nodes), 0) == lax.broadcasted_iota(
        jnp.int32, (nodes, nodes), 1
    )
    for batch in range(batches):
        here = slice(batch * nodes, (batch + 1) * nodes)
        count = adj[batch].astype(F32)
        hot = hot_rows(recv_row[...] - batch * nodes, nodes)
        degree = jnp.sum(count, axis=1, keepdims=True) + jnp.sum(hot, axis=1, keepdims=True)
        scale = 1.0 / (1.0 + degree)
        ratio[here] = scale
        ratio_row[:, here] = jnp.broadcast_to(scale, (nodes, 128)).T[:8]
        count = count + jnp.where(eye, 2.0, 0.0)
        adj_t[batch] = count.T.astype(BF16)
        count = count.astype(BF16)
        for at in tiles(feats.shape[1]):
            value = scale * jnp.dot(count, feats[here, at], preferred_element_type=F32)
            low = at.start % half
            mixed[at.start // half, here, low : low + at.stop - at.start] = value.astype(BF16)
            mixed_t[at, here] = value.T.astype(BF16)
    copies[3].wait()


def pre_own_kernel(place, mixed, weight, pre):
    me = place[0]
    for at in tiles(pre.shape[1]):
        pre[:, at] = jnp.dot(mixed[me], weight[:, at], preferred_element_type=F32)


def pre_other_kernel(place, before, mixed, weight, pre):
    me = place[0]
    for at in tiles(pre.shape[1]):
        pre[:, at] = before[:, at] + jnp.dot(mixed[1 - me], weight[:, at], preferred_element_type=F32)


def finish_kernel(axes, block, place, recv_row, ratio_row, mixed_t, *refs):
    pieces, (mine, theirs) = refs[:-2], refs[-2:]
    me, part = place[0], place[1]
    first = me == 0
    rows = mixed_t.shape[1]
    hot = hot_rows(recv_row[...], rows).T.astype(BF16)
    scale = ratio_row[0:1]
    for at in tiles(mixed_t.shape[0], 256):
        remote = jnp.dot(stack([piece.at[:, at] for piece in pieces]).T, hot, preferred_element_type=F32)
        value = (mixed_t[at].astype(F32) + scale * remote).reshape(128 // block, 2, block, rows)
        for out, swap in ((mine, False), (theirs, True)):
            low, high = (1, 0) if swap else (0, 1)
            chosen = jnp.where(first, value[:, low], value[:, high])
            if axes is None:
                out[at.start // 2 : at.stop // 2] = chosen.reshape(128, rows).astype(BF16)
                continue
            owner = 1 - me if swap else me
            for i in range(128 // block):
                spot = spot_of(axes, part, owner, at.start // (2 * block) + i)
                out[pl.ds(pl.multiple_of(spot * block, block), block)] = chosen[i].astype(BF16)


def remote_kernel(place, own, other, bias_own, bias_other, *refs):
    pieces, (out, bias) = refs[:-2], refs[-2:]
    half = own.shape[0]
    me = place[0]
    spots = out.shape[0] // 2
    here = stack([piece.at[:, pl.ds(pl.multiple_of(me * half, half), half)] for piece in pieces])
    there = stack([piece.at[:, pl.ds(pl.multiple_of((1 - me) * half, half), half)] for piece in pieces])
    for at in tiles(own.shape[1]):
        product = jnp.dot(here, own[:, at], preferred_element_type=F32)
        product += jnp.dot(there, other[:, at], preferred_element_type=F32)
        high = product.astype(BF16)
        out[:spots, at] = high
        out[spots:, at] = (product - high.astype(F32)).astype(BF16)
    mine, theirs = bias_own[...].astype(F32), bias_other[...].astype(F32)
    bias[:, :half] = jnp.where(me == 0, mine, theirs)
    bias[:, half:] = jnp.where(me == 0, theirs, mine)


def gelu_kernel(start, recv_row, ratio, remote, pre, bias, cot, act, dpre, bias_term, value, result, sems):
    rows, size = dpre.shape
    at = slice(start, start + size)
    hot = hot_rows(recv_row[...], rows).astype(BF16)
    value[...] = pre[:, at] + bias[:, at] + ratio[...] * jnp.dot(
        jnp.concatenate([hot, hot], axis=1), remote[:, at], preferred_element_type=F32
    )
    step = 64

    def body(i, total):
        here = pl.ds(pl.multiple_of(i * step, step), step)
        v = value[here]
        square = v * v
        left = 0.5 + 0.5 * jnp.tanh(v * (GELU_C + GELU_C * GELU_A * square))
        out = v * left
        result[here] = out.astype(BF16)
        slope = left + (out - out * left) * (2.0 * GELU_C + 6.0 * GELU_C * GELU_A * square)
        grad = (cot[here, at].astype(F32) * slope).astype(BF16)
        dpre[here] = grad
        return total + grad.astype(F32).reshape(step // 8, 8, size).sum(axis=0)

    total = jnp.zeros((8, size), F32)
    pieces = sems.shape[0]
    steps = rows // step
    copies = []
    for piece in range(pieces):
        low, high = piece * steps // pieces, (piece + 1) * steps // pieces
        total = lax.fori_loop(low, high, body, total)
        here = slice(low * step, high * step)
        copies.append(pltpu.make_async_copy(result.at[here], act.at[here, at], sems.at[piece]))
        copies[-1].start()
    bias_term[...] = jnp.sum(total, axis=0, keepdims=True)
    for copy in copies:
        copy.wait()


def spot_of(axes, part, owner, index):
    apart = turn_digits(part ^ index, owner)
    spot = 0
    for axis in axes:
        spot = spot * 2 + (lax.shift_right_logical(apart, axis) & 1)
    return spot


def grad_kernel(order, block, mine, theirs, dpre_mine, dpre_theirs, keep, leave):
    half = keep.shape[0]
    count = min(256 // block, len(order) // 2)
    for i in range(0, len(order), count):
        spots = [slice(spot * block, (spot + 1) * block) for spot in order[i : i + count]]
        total = jnp.dot(stack([mine.at[at] for at in spots]), dpre_mine[...], preferred_element_type=F32)
        total += jnp.dot(stack([theirs.at[at] for at in spots]), dpre_theirs[...], preferred_element_type=F32)
        low = i * block % half
        out = keep if i * block < half else leave
        out[low : low + count * block] = total.astype(BF16)


def sent_kernel(chunks, parts, per_part, sources, place, recv_row, ratio_row, *refs):
    dpres, bias_terms, outs = refs[:chunks], refs[chunks : 2 * chunks], refs[2 * chunks : -1]
    lines = refs[-1]
    width = lines.shape[1]
    rows = ratio_row.shape[1]
    hot = (hot_rows(recv_row[...], rows).T * ratio_row[0:1]).astype(BF16)
    me, part = place[0], place[1]
    size = outs[0].shape[0]
    start = 0
    for dpre in dpres:
        at = slice(start, start + dpre.shape[1])
        value = jnp.dot(hot, dpre[...], preferred_element_type=F32)
        for i, out in enumerate(outs):
            out[:, at] = value[i * size : (i + 1) * size].astype(BF16)
        start = at.stop
    bias = jnp.concatenate([term[...] for term in bias_terms], axis=1)
    high = bias.astype(BF16).astype(F32)
    middle = (bias - high).astype(BF16).astype(F32)
    line = lax.broadcasted_iota(jnp.int32, (8, width), 0)
    lines[...] = jnp.where(line == 0, high, jnp.where(line == 1, middle, bias - high - middle))
    count = width // parts
    line = lax.broadcasted_iota(jnp.int32, (8, count), 0)
    for i, out in enumerate(outs):
        pieces = []
        for source in sources[i]:
            if len(outs) > 1:
                to = part ^ turn_digits(source, 0 if DIRECT else me)
                piece = lines[:, pl.ds(pl.multiple_of(to * count, count), count)]
            else:
                piece = lines[:, source * count : (source + 1) * count]
            piece = jnp.where(line < 3, piece, 0.0)
            if count < 128:
                piece = jnp.concatenate([piece, jnp.zeros((8, 128 - count), F32)], axis=1)
            if per_part > 8:
                piece = jnp.concatenate([piece, jnp.zeros((per_part - 8, piece.shape[1]), F32)], axis=0)
            pieces.append(piece)
        out[:, width:] = jnp.concatenate(pieces, axis=0).astype(BF16)


def back_kernel(chunks, ratio, weight, *refs):
    dpres, out = refs[:chunks], refs[chunks]
    for at in tiles(weight.shape[0], 256):
        total = None
        start = 0
        for dpre in dpres:
            size = dpre.shape[1]
            term = lax.dot_general(dpre[...], weight[at, start : start + size], NT, preferred_element_type=F32)
            total = term if total is None else total + term
            start += size
        out[:, at] = (ratio[...] * total).astype(BF16)


def local_kernel(adj_t, dtotal, out):
    batches, nodes, _ = adj_t.shape
    for batch in range(batches):
        here = slice(batch * nodes, (batch + 1) * nodes)
        for at in tiles(dtotal.shape[1]):
            out[here, at] = jnp.dot(adj_t[batch], dtotal[here, at], preferred_element_type=F32)


def input_kernel(place, send_row, own, other, weight_own, weight_other, *refs):
    pieces, (out, result, sems) = refs[:-3], refs[-3:]
    rows, half = own.shape
    hot = hot_rows(send_row[...], rows).astype(BF16)
    grad = stack([piece.at[:, : 2 * half] for piece in pieces])
    me = place[0]
    copies = []
    for partial, weight, spot in ((own, weight_own, me), (other, weight_other, 1 - me)):
        for at in tiles(half):
            here = pl.ds(pl.multiple_of(spot * half + at.start, 512), at.stop - at.start)
            returned = lax.dot_general(grad, weight[at], NT, preferred_element_type=F32).astype(BF16)
            total = partial[:, at] + jnp.dot(hot, returned, preferred_element_type=F32)
            i = len(copies)
            result[i] = total.astype(BF16)
            copies.append(pltpu.make_async_copy(result.at[i], out.at[:, here], sems.at[i]))
            copies[-1].start()
    for copy in copies:
        copy.wait()


def bias_kernel(*refs):
    out = refs[-1]
    width = refs[0].shape[1] - out.shape[1]
    out[...] = sum(jnp.sum(piece[:, width:].astype(F32), axis=0, keepdims=True) for piece in refs[:-1])


def halve_kernel(*refs):
    pairs, (stay, leave) = refs[:-2], refs[-2:]
    half = stay.shape[0]
    for out, low in ((leave, half), (stay, 0)):
        here = slice(low, low + half)
        start = 0
        for keep, arrived in zip(pairs[::2], pairs[1::2]):
            at = slice(start, start + keep.shape[1])
            out[:, at] = (keep[here].astype(F32) + arrived[here].astype(F32)).astype(BF16)
            start = at.stop


def last_kernel(place, bias_mine, bias_theirs, *refs):
    out, bias_out = refs[-2:]
    start = 0
    for keep, arrived in zip(refs[:-2:2], refs[1:-2:2]):
        size = keep.shape[1]
        out[:, start : start + size] = keep[...].astype(F32) + arrived[...].astype(F32)
        start += size
    bias = bias_mine[...] + bias_theirs[...]
    count = bias_out.shape[1]
    bias_out[...] = jnp.where(place[0] == 0, bias[:, :count], bias[:, count : 2 * count])


def partners(parts, axis):
    turned = {0: 1, 1: 0}.get(axis, axis) if parts > 2 else axis
    return [(p * 2 + c, (p ^ (1 << (axis, turned)[c])) * 2 + c) for p in range(parts) for c in range(2)]


class Reduction:
    def __init__(self, order, parts, axes, keep, leave):
        self.order = order
        self.parts = parts
        self.axes = list(axes)
        self.send(keep, leave)

    def send(self, keep, leave):
        self.pairs = [(keep, lax.ppermute(leave, AXES, partners(self.parts, self.axes.pop(0))))]

    def join(self, other):
        self.pairs = other.pairs + self.pairs
        other.pairs = []

    def flat(self):
        return [x for pair in self.pairs for x in pair]

    def step(self):
        rows = self.pairs[0][0].shape[0]
        half = sds((rows // 2, sum(keep.shape[1] for keep, _ in self.pairs)), BF16)
        self.send(*self.order.run(halve_kernel, "halve", (half, half), self.flat()))


class Exchange:
    def __init__(self, order, parts, axes, size, pieces):
        self.order, self.parts, self.axes, self.size = order, parts, list(axes), size
        self.lists = halves(range(parts), self.axes[0])
        self.stay, leave = pieces
        self.arrived = lax.ppermute(leave, AXES, partners(parts, self.axes.pop(0)))

    def step(self):
        if not self.axes:
            return
        found = {r: (i, spot) for i in range(2) for spot, r in enumerate(self.lists[i])}
        axis = self.axes.pop(0)
        self.lists = halves(self.lists[0] + self.lists[1], axis)
        orders = [[found[r] for r in part] for part in self.lists]
        shape = sds(self.stay.shape, BF16)
        self.stay, leave = self.order.run(
            functools.partial(regroup_kernel, self.size, orders), "regroup", (shape, shape), (self.stay, self.arrived)
        )
        self.arrived = lax.ppermute(leave, AXES, partners(self.parts, axis))


def halves(distances, axis):
    return [[r for r in distances if (r >> axis) & 1 == side] for side in range(2)]


def local(parts, features, weight, bias, local_adj, send_index, recv_target, cotangent):
    batches, nodes, width = features.shape
    rows = batches * nodes
    half = width // 2
    core = lax.axis_index("mp").astype(jnp.int32)
    part = lax.axis_index("parts").astype(jnp.int32)
    place = jnp.stack([core, part])
    paired = parts & (parts - 1) == 0 and width % (2 * parts) == 0 and (width // (2 * parts)) % 16 == 0
    block = width // (2 * parts)

    feats = features.reshape(rows, width)
    cot = cotangent.reshape(rows, width)
    digits = parts.bit_length() - 1
    near = min(4, parts)
    far = parts // near
    orders = [None] * 4
    early = late = None
    if paired:
        late = list(range(digits))
        early = late[2:] + late[:2]
        back = [axis for axis in BACK if axis < digits] + list(range(len(BACK), digits))
        first, last = halves(range(parts), back[0]), list(range(parts))
        for axis in back:
            last = sum(halves(last, axis), [])
        across = [k * near + j for j in range(near) for k in range(far)]
        orders = [list(range(parts)), across, sum(first, []), last]
        if DIRECT:
            orders[2:] = [list(range(parts)), across]
            first = [[k * near + j for j in range(near)] for k in range(far)]
    slots = send_index.size
    per_part = slots // parts

    def move(pieces, stride):
        moved = list(pieces)
        for i in range(1, len(pieces)) if stride > 1 else reversed(range(1, len(pieces))):
            perm = [(p, p ^ (i * stride)) for p in range(parts)]
            moved[i] = lax.ppermute(pieces[i], "parts", perm)
        return moved

    def exchange(values):
        moved = lax.all_to_all(
            values.reshape(parts, per_part, values.shape[1]), "parts", split_axis=0, concat_axis=0, tiled=True
        )
        return moved.reshape(values.shape)

    other = lax.ppermute(weight, "mp", SWAP)
    bias_own = bias.reshape(1, half)
    bias_other = lax.ppermute(bias_own, "mp", SWAP)
    order = Order(12 if paired else 48)
    run = order.run
    turn = (0, 1, 3, 2)
    pieces = far if paired else 1
    turned = jnp.transpose(send_index, turn), jnp.transpose(recv_target, turn)
    indices = [pltpu.VMEM(x.shape, jnp.int32) for x in turned]
    feats, *outgoing = run(
        functools.partial(outgoing_kernel, nodes, orders[0]),
        "outgoing",
        (sds((rows, width), BF16),) + (sds((slots // pieces, width), BF16),) * pieces,
        (),
        scalars=(place,),
        far=(feats, turned[0]),
        scratch=[indices[0], pltpu.SemaphoreType.DMA((5,))],
    )
    if paired:
        outgoing = move(outgoing, near)

    row = sds((1, slots), jnp.int32)
    order.cost = 6 * 10**10
    mixed, mixed_t, ratio, ratio_row, adj_t, weight, send_row, recv_row, back_row = run(
        functools.partial(mix_kernel, orders),
        "mix",
        (
            sds((2, rows, half), BF16),
            sds((width, rows), BF16),
            sds((rows, 1), F32),
            sds((8, rows), F32),
            sds((batches, nodes, nodes), BF16),
            sds(weight.shape, BF16),
            row,
            row,
            row,
        ),
        (feats,),
        scalars=(place,),
        far=(weight, local_adj, *turned),
        scratch=[pltpu.VMEM(local_adj.shape, jnp.int32), *indices, pltpu.SemaphoreType.DMA((4,))],
    )
    order.cost = 1
    (pre,) = run(pre_own_kernel, "pre_own", (sds((rows, width), F32),), (mixed, weight), scalars=(place,))
    if paired:
        arrived = run(
            functools.partial(
                regroup_kernel, per_part, [[(k, j) for k in range(far)] for j in range(near)]
            ),
            "regroup",
            (sds((far * per_part, width), BF16),) * near,
            outgoing,
        )
        arrived = move(arrived, 1)
    else:
        arrived = [exchange(outgoing[0])]
    (pre,) = run(
        pre_other_kernel, "pre_other", (sds((rows, width), F32),), (pre, mixed, other), scalars=(place,)
    )
    remote, bias_full = run(
        remote_kernel,
        "remote_product",
        (sds((2 * slots, width), BF16), sds((1, width), F32)),
        (weight, other, bias_own, bias_other, *arrived),
        scalars=(place,),
    )

    starts = [sum(CHUNKS[:i]) for i in range(len(CHUNKS))]
    act = None
    dpres, dpres_other, bias_terms, sums, dtotals, partials = [], [], [], [], [], []

    def gelu(i):
        nonlocal act
        size = CHUNKS[i]
        act, dpre, bias_term = run(
            functools.partial(gelu_kernel, starts[i]),
            "gelu",
            (sds((rows, width), BF16), sds((rows, size), BF16), sds((1, size), F32)),
            (recv_row, ratio, remote, pre, bias_full, cot),
            scratch=[pltpu.VMEM((rows, size), F32), pltpu.VMEM((rows, size), BF16), pltpu.SemaphoreType.DMA((3,))],
            keep=act,
        )
        dpres.append(dpre)
        dpres_other.append(lax.ppermute(dpre, "mp", SWAP))
        bias_terms.append(bias_term)

    def grad(i, mine, theirs):
        size = CHUNKS[i]
        shape = sds((half // 2, size), BF16)
        if paired:
            axes = early if i == FAR_FIRST else late
            spots = [sum(((r >> axes[::-1].index(axis)) & 1) << d for d, axis in enumerate(late[::-1])) for r in range(parts)]
            size_of = block
        else:
            spots, size_of = list(range(half // 128)), 128
        keep, leave = run(
            functools.partial(grad_kernel, spots, size_of),
            "grad",
            (shape, shape),
            (mine, theirs, dpres[i], dpres_other[i]),
        )
        if paired:
            sums.append(Reduction(order, parts, axes, keep, leave))
            return
        both = jnp.concatenate([keep, leave]).astype(F32)
        sums.append(lax.psum_scatter(both, "parts", scatter_dimension=0, tiled=True))

    extra = max(128, width // parts)
    pieces = (far if DIRECT else 2) if paired else 1
    for step, cost in zip(PLAN, COSTS):
        kind, number = step[0], int(step[1:] or 0)
        order.cost = cost
        if kind == "g":
            gelu(number)
        elif kind == "f":
            mine, theirs = run(
                functools.partial(finish_kernel, late, block),
                "finish_mixed",
                (sds((half, rows), BF16), sds((half, rows), BF16)),
                (recv_row, ratio_row, mixed_t, *arrived),
                scalars=(place,),
            )
            theirs = lax.ppermute(theirs, "mp", SWAP)
        elif kind == "d":
            grad(number, mine, theirs)
        elif kind == "s":
            sent = run(
                functools.partial(
                    sent_kernel, len(CHUNKS), parts, per_part, first if paired else [list(range(parts))]
                ),
                "sent_grads",
                (sds((slots // pieces, width + extra), BF16),) * pieces,
                (back_row, ratio_row, *dpres, *bias_terms),
                scalars=(place,),
                scratch=[pltpu.VMEM((8, width), F32)],
            )
            if paired:
                swap = move(sent, near) if DIRECT else Exchange(order, parts, back, per_part, sent)
            else:
                returned = [exchange(sent[0])]
        elif kind == "b":
            (dtotal,) = run(
                functools.partial(back_kernel, len(CHUNKS)),
                "back",
                (sds((rows, half), BF16),),
                (ratio, (weight, other)[number], *dpres),
            )
            dtotals.append(dtotal)
        elif kind == "l":
            (partial,) = run(local_kernel, "input_local", (sds((rows, half), F32),), (adj_t, dtotals[number]))
            partials.append(partial)
        elif kind == "i":
            if paired:
                returned = swap if DIRECT else [swap.stay, swap.arrived]
            (bias_mine,) = run(bias_kernel, "bias_sum", (sds((1, extra), F32),), returned)
            bias_theirs = lax.ppermute(bias_mine, "mp", SWAP)
            size = min(512, half)
            (input_grad,) = run(
                input_kernel,
                "input_gradient",
                (sds((rows, width), BF16),),
                (send_row, *partials, weight, other, *returned),
                scalars=(place,),
                scratch=[pltpu.VMEM((width // size, rows, size), BF16), pltpu.SemaphoreType.DMA((width // size,))],
                keep=None,
            )
        elif paired and kind == "r":
            if JOIN and number == 1 and len(sums[1].axes) == digits - 2:
                sums[1].join(sums[0])
            sums[number].step()
        elif paired and kind == "e":
            if DIRECT:
                swap = move(
                    run(
                        functools.partial(regroup_kernel, per_part, [[(k, j) for k in range(far)] for j in range(near)]),
                        "regroup",
                        (sds((far * per_part, width + extra), BF16),) * near,
                        swap,
                    ),
                    1,
                )
            else:
                swap.step()
    count = width // (2 * parts)
    if paired:
        weight_grad, bias_grad = run(
            last_kernel,
            "last_sum",
            (sds((block, width), F32), sds((1, count), F32)),
            [bias_mine, bias_theirs] + sum((s.flat() for s in sums), []),
            scalars=(place,),
        )
        bias_grad = bias_grad.reshape(count)
    else:
        weight_grad = jnp.concatenate(sums, axis=1)
        bias_all = (bias_mine + bias_theirs)[0]
        bias_grad = jnp.where(core == 0, bias_all[:count], bias_all[count : 2 * count])
    return (
        act.reshape(batches, nodes, width),
        input_grad.reshape(batches, nodes, width),
        weight_grad,
        bias_grad,
    )


def solution(mesh):
    return jax.shard_map(
        functools.partial(local, mesh.shape["parts"]),
        mesh=mesh,
        in_specs=(
            P("mp", "parts", None),
            P("mp", None),
            P("mp"),
            P("mp", "parts", None),
            P("mp", "parts", None, None),
            P("mp", "parts", None, None),
            P("mp", "parts", None),
        ),
        out_specs=(
            P("mp", "parts", None),
            P("mp", "parts", None),
            P(("parts", "mp"), None),
            P(("parts", "mp")),
        ),
        check_vma=False,
    )
```

```python
import functools
import math

import jax
import jax.numpy as jnp
from jax import lax
from jax.experimental import pallas as pl
from jax.experimental.pallas import tpu as pltpu
from jax.sharding import PartitionSpec as P

F32 = jnp.float32
BF16 = jnp.bfloat16
AXES = ("parts", "mp")
SWAP = ((0, 1), (1, 0))
GELU_C = math.sqrt(2.0 / math.pi)
GELU_A = 0.044715
CHUNKS = (1024, 768, 256)
FAR_FIRST = 2
BACK = (3, 2, 0, 1)
DIRECT = True
JOIN = False
PLAN = ('f', 'g0', 'g1', 'g2', 's', 'd0', 'd1', 'd2', 'b0', 'b1', 'e', 'r0', 'r2', 'l0', 'r1', 'r0', 'r2', 'r1', 'r2', 'r0', 'l1', 'r1', 'i')
COSTS = (16000000000, 8500000000, 2000000000, 1500000000, 1, 10500000000, 1, 1, 1, 1, 1000000000, 1000000000, 4000000000, 1, 1, 1, 4000000000, 1, 1, 1000000000, 1000000000, 1, 1000000000)
VMEM = pl.BlockSpec(memory_space=pltpu.VMEM)
SMEM = pl.BlockSpec(memory_space=pltpu.SMEM)
ANY = pl.BlockSpec(memory_space=pl.ANY)
HBM = pl.BlockSpec(memory_space=pltpu.HBM)
NT = (((1,), (1,)), ((), ()))


def sds(shape, dtype):
    return jax.ShapeDtypeStruct(shape, dtype)


class Order:
    def __init__(self, limit):
        self.token = None
        self.limit = limit
        self.cost = 1

    def run(self, kernel, name, out_shape, args, scalars=(), far=(), scratch=(), keep=False):
        specs = [SMEM] * len(scalars) + [HBM] * len(far) + [VMEM] * len(args)
        args = [*scalars, *(pltpu.with_memory_space_constraint(x, pltpu.HBM) for x in far), *args]
        used = len(args)
        aliases = {}
        if keep is not None and keep is not False:
            aliases = {len(args): 0}
            args.append(keep)
            specs.append(ANY)
        if self.token is not None:
            args.append(self.token)
            specs.append(VMEM)
        count, results = len(args), len(out_shape)

        def body(*refs):
            refs[count + results][...] = jnp.zeros((8, 128), F32)
            kernel(*refs[:used], *refs[count : count + results], *refs[count + results + 1 :])

        *out, self.token = pl.pallas_call(
            body,
            name=name,
            in_specs=specs,
            out_specs=((VMEM if keep is False else ANY,) + (VMEM,) * results),
            out_shape=(*out_shape, sds((8, 128), F32)),
            scratch_shapes=scratch,
            input_output_aliases=aliases,
            compiler_params=pltpu.CompilerParams(vmem_limit_bytes=self.limit * 2**20),
            cost_estimate=pl.CostEstimate(flops=self.cost, bytes_accessed=1, transcendentals=0),
        )(*args)
        return out


def hot_rows(index_row, rows):
    match = lax.broadcasted_iota(jnp.int32, (rows, index_row.shape[1]), 0) == index_row
    return jnp.where(match, 1.0, 0.0)


def tiles(width, size=512):
    return [slice(i, min(i + size, width)) for i in range(0, width, size)]


def index_column(index, part, nodes, order=None, turned=0):
    batches, _, depth, parts = index.shape
    slots = batches * parts * depth
    slot = lax.broadcasted_iota(jnp.int32, (slots, parts), 0)
    spot, rest = lax.div(slot, batches * depth), lax.rem(slot, batches * depth)
    if order is not None:
        apart = jnp.zeros((slots, parts), jnp.int32)
        for i, distance in enumerate(order):
            apart = jnp.where(spot == i, distance, apart)
        spot = turn_digits(apart, turned) ^ part
    here = lax.broadcasted_iota(jnp.int32, (slots, parts), 1) == spot
    total = jnp.zeros((slots, parts), jnp.int32)
    for batch in range(batches):
        node = index[batch, 0]
        node = jnp.where(node < 0, -1, node + batch * nodes)
        for h in range(depth):
            total = jnp.where(rest == batch * depth + h, node[h : h + 1], total)
    return jnp.sum(jnp.where(here, total, 0), axis=1, keepdims=True)


def turn_digits(value, turned):
    differ = (value ^ lax.shift_right_logical(value, 1)) & turned
    return value ^ differ ^ (differ << 1)


def as_row(column):
    return jnp.broadcast_to(column, (column.shape[0], 128)).T[:1]


def hot_cols(index_col, cols):
    match = lax.broadcasted_iota(jnp.int32, (index_col.shape[0], cols), 1) == index_col
    return jnp.where(match, 1.0, 0.0)


def outgoing_kernel(nodes, order, place, feats, send_far, here, *rest):
    outs, (send, sems) = rest[:-2], rest[-2:]
    width = feats.shape[1]
    ranges = tiles(width, width // (sems.shape[0] - 1))
    copies = [pltpu.make_async_copy(feats.at[:, at], here.at[:, at], sems.at[i]) for i, at in enumerate(ranges)]
    fetch = pltpu.make_async_copy(send_far, send, sems.at[len(ranges)])
    for copy in (fetch, *copies):
        copy.start()
    fetch.wait()
    hot = hot_cols(index_column(send, place[1], nodes, order), feats.shape[0]).astype(BF16)
    size = outs[0].shape[0]
    for at, copy in zip(ranges, copies):
        copy.wait()
        value = jnp.dot(hot, here[:, at], preferred_element_type=F32)
        for i, out in enumerate(outs):
            out[:, at] = value[i * size : (i + 1) * size].astype(BF16)


def regroup_kernel(size, orders, *refs):
    pieces, outs = refs[: -len(orders)], refs[-len(orders) :]
    values = [piece[...].astype(F32) for piece in pieces]
    for order, out in zip(orders, outs):
        blocks = [values[i][block * size : (block + 1) * size] for i, block in order]
        out[...] = jnp.concatenate(blocks, axis=0).astype(BF16)


def stack(pieces):
    return jnp.concatenate([piece[...] for piece in pieces], axis=0)


def mix_kernel(orders, place, weight, edges, send_far, recv_far, feats, *refs):
    mixed, mixed_t, ratio, ratio_row, adj_t, own, send_row, recv_row, back_row, adj, send, recv, sems = refs
    copies = [
        pltpu.make_async_copy(source, target, sems.at[i])
        for i, (source, target) in enumerate(((recv_far, recv), (send_far, send), (edges, adj), (weight, own)))
    ]
    for copy in copies:
        copy.start()
    for copy in copies[:3]:
        copy.wait()
    me, part = place[0], place[1]
    nodes = adj.shape[1]
    recv_row[...] = as_row(index_column(recv, part, nodes, orders[1]))
    back_row[...] = as_row(index_column(recv, part, nodes, orders[2], 0 if DIRECT else me))
    send_row[...] = as_row(index_column(send, part, nodes, orders[3], 0 if DIRECT else me))
    batches, nodes, _ = adj.shape
    half = mixed.shape[2]
    eye = lax.broadcasted_iota(jnp.int32, (nodes, nodes), 0) == lax.broadcasted_iota(
        jnp.int32, (nodes, nodes), 1
    )
    for batch in range(batches):
        here = slice(batch * nodes, (batch + 1) * nodes)
        count = adj[batch].astype(F32)
        hot = hot_rows(recv_row[...] - batch * nodes, nodes)
        degree = jnp.sum(count, axis=1, keepdims=True) + jnp.sum(hot, axis=1, keepdims=True)
        scale = 1.0 / (1.0 + degree)
        ratio[here] = scale
        ratio_row[:, here] = jnp.broadcast_to(scale, (nodes, 128)).T[:8]
        count = count + jnp.where(eye, 2.0, 0.0)
        adj_t[batch] = count.T.astype(BF16)
        count = count.astype(BF16)
        for at in tiles(feats.shape[1]):
            value = scale * jnp.dot(count, feats[here, at], preferred_element_type=F32)
            low = at.start % half
            mixed[at.start // half, here, low : low + at.stop - at.start] = value.astype(BF16)
            mixed_t[at, here] = value.T.astype(BF16)
    copies[3].wait()


def pre_own_kernel(place, mixed, weight, pre):
    me = place[0]
    for at in tiles(pre.shape[1]):
        pre[:, at] = jnp.dot(mixed[me], weight[:, at], preferred_element_type=F32)


def pre_other_kernel(place, before, mixed, weight, pre):
    me = place[0]
    for at in tiles(pre.shape[1]):
        pre[:, at] = before[:, at] + jnp.dot(mixed[1 - me], weight[:, at], preferred_element_type=F32)


def finish_kernel(axes, block, place, recv_row, ratio_row, mixed_t, *refs):
    pieces, (mine, theirs) = refs[:-2], refs[-2:]
    me, part = place[0], place[1]
    first = me == 0
    rows = mixed_t.shape[1]
    hot = hot_rows(recv_row[...], rows).T.astype(BF16)
    scale = ratio_row[0:1]
    for at in tiles(mixed_t.shape[0], 256):
        remote = jnp.dot(stack([piece.at[:, at] for piece in pieces]).T, hot, preferred_element_type=F32)
        value = (mixed_t[at].astype(F32) + scale * remote).reshape(128 // block, 2, block, rows)
        for out, swap in ((mine, False), (theirs, True)):
            low, high = (1, 0) if swap else (0, 1)
            chosen = jnp.where(first, value[:, low], value[:, high])
            if axes is None:
                out[at.start // 2 : at.stop // 2] = chosen.reshape(128, rows).astype(BF16)
                continue
            owner = 1 - me if swap else me
            for i in range(128 // block):
                spot = spot_of(axes, part, owner, at.start // (2 * block) + i)
                out[pl.ds(pl.multiple_of(spot * block, block), block)] = chosen[i].astype(BF16)


def remote_kernel(place, own, other, bias_own, bias_other, *refs):
    pieces, (out, bias) = refs[:-2], refs[-2:]
    half = own.shape[0]
    me = place[0]
    spots = out.shape[0] // 2
    here = stack([piece.at[:, pl.ds(pl.multiple_of(me * half, half), half)] for piece in pieces])
    there = stack([piece.at[:, pl.ds(pl.multiple_of((1 - me) * half, half), half)] for piece in pieces])
    for at in tiles(own.shape[1]):
        product = jnp.dot(here, own[:, at], preferred_element_type=F32)
        product += jnp.dot(there, other[:, at], preferred_element_type=F32)
        high = product.astype(BF16)
        out[:spots, at] = high
        out[spots:, at] = (product - high.astype(F32)).astype(BF16)
    mine, theirs = bias_own[...].astype(F32), bias_other[...].astype(F32)
    bias[:, :half] = jnp.where(me == 0, mine, theirs)
    bias[:, half:] = jnp.where(me == 0, theirs, mine)


def gelu_kernel(start, recv_row, ratio, remote, pre, bias, cot, act, dpre, bias_term, value, result, sems):
    rows, size = dpre.shape
    at = slice(start, start + size)
    hot = hot_rows(recv_row[...], rows).astype(BF16)
    value[...] = pre[:, at] + bias[:, at] + ratio[...] * jnp.dot(
        jnp.concatenate([hot, hot], axis=1), remote[:, at], preferred_element_type=F32
    )
    step = 64

    def body(i, total):
        here = pl.ds(pl.multiple_of(i * step, step), step)
        v = value[here]
        square = v * v
        left = 0.5 + 0.5 * jnp.tanh(v * (GELU_C + GELU_C * GELU_A * square))
        out = v * left
        result[here] = out.astype(BF16)
        slope = left + (out - out * left) * (2.0 * GELU_C + 6.0 * GELU_C * GELU_A * square)
        grad = (cot[here, at].astype(F32) * slope).astype(BF16)
        dpre[here] = grad
        return total + grad.astype(F32).reshape(step // 8, 8, size).sum(axis=0)

    total = jnp.zeros((8, size), F32)
    pieces = sems.shape[0]
    steps = rows // step
    copies = []
    for piece in range(pieces):
        low, high = piece * steps // pieces, (piece + 1) * steps // pieces
        total = lax.fori_loop(low, high, body, total)
        here = slice(low * step, high * step)
        copies.append(pltpu.make_async_copy(result.at[here], act.at[here, at], sems.at[piece]))
        copies[-1].start()
    bias_term[...] = jnp.sum(total, axis=0, keepdims=True)
    for copy in copies:
        copy.wait()


def spot_of(axes, part, owner, index):
    apart = turn_digits(part ^ index, owner)
    spot = 0
    for axis in axes:
        spot = spot * 2 + (lax.shift_right_logical(apart, axis) & 1)
    return spot


def grad_kernel(order, block, mine, theirs, dpre_mine, dpre_theirs, keep, leave):
    half = keep.shape[0]
    count = min(256 // block, len(order) // 2)
    for i in range(0, len(order), count):
        spots = [slice(spot * block, (spot + 1) * block) for spot in order[i : i + count]]
        total = jnp.dot(stack([mine.at[at] for at in spots]), dpre_mine[...], preferred_element_type=F32)
        total += jnp.dot(stack([theirs.at[at] for at in spots]), dpre_theirs[...], preferred_element_type=F32)
        low = i * block % half
        out = keep if i * block < half else leave
        out[low : low + count * block] = total.astype(BF16)


def sent_kernel(chunks, parts, per_part, sources, place, recv_row, ratio_row, *refs):
    dpres, bias_terms, outs = refs[:chunks], refs[chunks : 2 * chunks], refs[2 * chunks : -1]
    lines = refs[-1]
    width = lines.shape[1]
    rows = ratio_row.shape[1]
    hot = (hot_rows(recv_row[...], rows).T * ratio_row[0:1]).astype(BF16)
    me, part = place[0], place[1]
    size = outs[0].shape[0]
    start = 0
    for dpre in dpres:
        at = slice(start, start + dpre.shape[1])
        value = jnp.dot(hot, dpre[...], preferred_element_type=F32)
        for i, out in enumerate(outs):
            out[:, at] = value[i * size : (i + 1) * size].astype(BF16)
        start = at.stop
    bias = jnp.concatenate([term[...] for term in bias_terms], axis=1)
    high = bias.astype(BF16).astype(F32)
    middle = (bias - high).astype(BF16).astype(F32)
    line = lax.broadcasted_iota(jnp.int32, (8, width), 0)
    lines[...] = jnp.where(line == 0, high, jnp.where(line == 1, middle, bias - high - middle))
    count = width // parts
    line = lax.broadcasted_iota(jnp.int32, (8, count), 0)
    for i, out in enumerate(outs):
        pieces = []
        for source in sources[i]:
            if len(outs) > 1:
                to = part ^ turn_digits(source, 0 if DIRECT else me)
                piece = lines[:, pl.ds(pl.multiple_of(to * count, count), count)]
            else:
                piece = lines[:, source * count : (source + 1) * count]
            piece = jnp.where(line < 3, piece, 0.0)
            if count < 128:
                piece = jnp.concatenate([piece, jnp.zeros((8, 128 - count), F32)], axis=1)
            if per_part > 8:
                piece = jnp.concatenate([piece, jnp.zeros((per_part - 8, piece.shape[1]), F32)], axis=0)
            pieces.append(piece)
        out[:, width:] = jnp.concatenate(pieces, axis=0).astype(BF16)


def back_kernel(chunks, ratio, weight, *refs):
    dpres, out = refs[:chunks], refs[chunks]
    for at in tiles(weight.shape[0], 256):
        total = None
        start = 0
        for dpre in dpres:
            size = dpre.shape[1]
            term = lax.dot_general(dpre[...], weight[at, start : start + size], NT, preferred_element_type=F32)
            total = term if total is None else total + term
            start += size
        out[:, at] = (ratio[...] * total).astype(BF16)


def local_kernel(adj_t, dtotal, out):
    batches, nodes, _ = adj_t.shape
    for batch in range(batches):
        here = slice(batch * nodes, (batch + 1) * nodes)
        for at in tiles(dtotal.shape[1]):
            out[here, at] = jnp.dot(adj_t[batch], dtotal[here, at], preferred_element_type=F32)


def input_kernel(place, send_row, own, other, weight_own, weight_other, *refs):
    pieces, (out, result, sems) = refs[:-3], refs[-3:]
    rows, half = own.shape
    hot = hot_rows(send_row[...], rows).astype(BF16)
    grad = stack([piece.at[:, : 2 * half] for piece in pieces])
    me = place[0]
    copies = []
    for partial, weight, spot in ((own, weight_own, me), (other, weight_other, 1 - me)):
        for at in tiles(half):
            here = pl.ds(pl.multiple_of(spot * half + at.start, 512), at.stop - at.start)
            returned = lax.dot_general(grad, weight[at], NT, preferred_element_type=F32).astype(BF16)
            total = partial[:, at] + jnp.dot(hot, returned, preferred_element_type=F32)
            i = len(copies)
            result[i] = total.astype(BF16)
            copies.append(pltpu.make_async_copy(result.at[i], out.at[:, here], sems.at[i]))
            copies[-1].start()
    for copy in copies:
        copy.wait()


def bias_kernel(*refs):
    out = refs[-1]
    width = refs[0].shape[1] - out.shape[1]
    out[...] = sum(jnp.sum(piece[:, width:].astype(F32), axis=0, keepdims=True) for piece in refs[:-1])


def halve_kernel(*refs):
    pairs, (stay, leave) = refs[:-2], refs[-2:]
    half = stay.shape[0]
    for out, low in ((leave, half), (stay, 0)):
        here = slice(low, low + half)
        start = 0
        for keep, arrived in zip(pairs[::2], pairs[1::2]):
            at = slice(start, start + keep.shape[1])
            out[:, at] = (keep[here].astype(F32) + arrived[here].astype(F32)).astype(BF16)
            start = at.stop


def last_kernel(place, bias_mine, bias_theirs, *refs):
    out, bias_out = refs[-2:]
    start = 0
    for keep, arrived in zip(refs[:-2:2], refs[1:-2:2]):
        size = keep.shape[1]
        out[:, start : start + size] = keep[...].astype(F32) + arrived[...].astype(F32)
        start += size
    bias = bias_mine[...] + bias_theirs[...]
    count = bias_out.shape[1]
    bias_out[...] = jnp.where(place[0] == 0, bias[:, :count], bias[:, count : 2 * count])


def partners(parts, axis):
    turned = {0: 1, 1: 0}.get(axis, axis) if parts > 2 else axis
    return [(p * 2 + c, (p ^ (1 << (axis, turned)[c])) * 2 + c) for p in range(parts) for c in range(2)]


class Reduction:
    def __init__(self, order, parts, axes, keep, leave):
        self.order = order
        self.parts = parts
        self.axes = list(axes)
        self.send(keep, leave)

    def send(self, keep, leave):
        self.pairs = [(keep, lax.ppermute(leave, AXES, partners(self.parts, self.axes.pop(0))))]

    def join(self, other):
        self.pairs = other.pairs + self.pairs
        other.pairs = []

    def flat(self):
        return [x for pair in self.pairs for x in pair]

    def step(self):
        rows = self.pairs[0][0].shape[0]
        half = sds((rows // 2, sum(keep.shape[1] for keep, _ in self.pairs)), BF16)
        self.send(*self.order.run(halve_kernel, "halve", (half, half), self.flat()))


class Exchange:
    def __init__(self, order, parts, axes, size, pieces):
        self.order, self.parts, self.axes, self.size = order, parts, list(axes), size
        self.lists = halves(range(parts), self.axes[0])
        self.stay, leave = pieces
        self.arrived = lax.ppermute(leave, AXES, partners(parts, self.axes.pop(0)))

    def step(self):
        if not self.axes:
            return
        found = {r: (i, spot) for i in range(2) for spot, r in enumerate(self.lists[i])}
        axis = self.axes.pop(0)
        self.lists = halves(self.lists[0] + self.lists[1], axis)
        orders = [[found[r] for r in part] for part in self.lists]
        shape = sds(self.stay.shape, BF16)
        self.stay, leave = self.order.run(
            functools.partial(regroup_kernel, self.size, orders), "regroup", (shape, shape), (self.stay, self.arrived)
        )
        self.arrived = lax.ppermute(leave, AXES, partners(self.parts, axis))


def halves(distances, axis):
    return [[r for r in distances if (r >> axis) & 1 == side] for side in range(2)]


def local(parts, features, weight, bias, local_adj, send_index, recv_target, cotangent):
    batches, nodes, width = features.shape
    rows = batches * nodes
    half = width // 2
    core = lax.axis_index("mp").astype(jnp.int32)
    part = lax.axis_index("parts").astype(jnp.int32)
    place = jnp.stack([core, part])
    paired = parts & (parts - 1) == 0 and width % (2 * parts) == 0 and (width // (2 * parts)) % 16 == 0
    block = width // (2 * parts)

    feats = features.reshape(rows, width)
    cot = cotangent.reshape(rows, width)
    digits = parts.bit_length() - 1
    near = min(4, parts)
    far = parts // near
    orders = [None] * 4
    early = late = None
    if paired:
        late = list(range(digits))
        early = late[2:] + late[:2]
        back = [axis for axis in BACK if axis < digits] + list(range(len(BACK), digits))
        first, last = halves(range(parts), back[0]), list(range(parts))
        for axis in back:
            last = sum(halves(last, axis), [])
        across = [k * near + j for j in range(near) for k in range(far)]
        orders = [list(range(parts)), across, sum(first, []), last]
        if DIRECT:
            orders[2:] = [list(range(parts)), across]
            first = [[k * near + j for j in range(near)] for k in range(far)]
    slots = send_index.size
    per_part = slots // parts

    def move(pieces, stride):
        moved = list(pieces)
        for i in reversed(range(1, len(pieces))):
            perm = [(p, p ^ (i * stride)) for p in range(parts)]
            moved[i] = lax.ppermute(pieces[i], "parts", perm)
        return moved

    def exchange(values):
        moved = lax.all_to_all(
            values.reshape(parts, per_part, values.shape[1]), "parts", split_axis=0, concat_axis=0, tiled=True
        )
        return moved.reshape(values.shape)

    other = lax.ppermute(weight, "mp", SWAP)
    bias_own = bias.reshape(1, half)
    bias_other = lax.ppermute(bias_own, "mp", SWAP)
    order = Order(12 if paired else 48)
    run = order.run
    turn = (0, 1, 3, 2)
    pieces = far if paired else 1
    turned = jnp.transpose(send_index, turn), jnp.transpose(recv_target, turn)
    indices = [pltpu.VMEM(x.shape, jnp.int32) for x in turned]
    feats, *outgoing = run(
        functools.partial(outgoing_kernel, nodes, orders[0]),
        "outgoing",
        (sds((rows, width), BF16),) + (sds((slots // pieces, width), BF16),) * pieces,
        (),
        scalars=(place,),
        far=(feats, turned[0]),
        scratch=[indices[0], pltpu.SemaphoreType.DMA((5,))],
    )
    if paired:
        outgoing = move(outgoing, near)

    row = sds((1, slots), jnp.int32)
    order.cost = 6 * 10**10
    mixed, mixed_t, ratio, ratio_row, adj_t, weight, send_row, recv_row, back_row = run(
        functools.partial(mix_kernel, orders),
        "mix",
        (
            sds((2, rows, half), BF16),
            sds((width, rows), BF16),
            sds((rows, 1), F32),
            sds((8, rows), F32),
            sds((batches, nodes, nodes), BF16),
            sds(weight.shape, BF16),
            row,
            row,
            row,
        ),
        (feats,),
        scalars=(place,),
        far=(weight, local_adj, *turned),
        scratch=[pltpu.VMEM(local_adj.shape, jnp.int32), *indices, pltpu.SemaphoreType.DMA((4,))],
    )
    order.cost = 1
    (pre,) = run(pre_own_kernel, "pre_own", (sds((rows, width), F32),), (mixed, weight), scalars=(place,))
    if paired:
        arrived = run(
            functools.partial(
                regroup_kernel, per_part, [[(k, j) for k in range(far)] for j in range(near)]
            ),
            "regroup",
            (sds((far * per_part, width), BF16),) * near,
            outgoing,
        )
        arrived = move(arrived, 1)
    else:
        arrived = [exchange(outgoing[0])]
    (pre,) = run(
        pre_other_kernel, "pre_other", (sds((rows, width), F32),), (pre, mixed, other), scalars=(place,)
    )
    remote, bias_full = run(
        remote_kernel,
        "remote_product",
        (sds((2 * slots, width), BF16), sds((1, width), F32)),
        (weight, other, bias_own, bias_other, *arrived),
        scalars=(place,),
    )

    starts = [sum(CHUNKS[:i]) for i in range(len(CHUNKS))]
    act = None
    dpres, dpres_other, bias_terms, sums, dtotals, partials = [], [], [], [], [], []

    def gelu(i):
        nonlocal act
        size = CHUNKS[i]
        act, dpre, bias_term = run(
            functools.partial(gelu_kernel, starts[i]),
            "gelu",
            (sds((rows, width), BF16), sds((rows, size), BF16), sds((1, size), F32)),
            (recv_row, ratio, remote, pre, bias_full, cot),
            scratch=[pltpu.VMEM((rows, size), F32), pltpu.VMEM((rows, size), BF16), pltpu.SemaphoreType.DMA((3,))],
            keep=act,
        )
        dpres.append(dpre)
        dpres_other.append(lax.ppermute(dpre, "mp", SWAP))
        bias_terms.append(bias_term)

    def grad(i, mine, theirs):
        size = CHUNKS[i]
        shape = sds((half // 2, size), BF16)
        if paired:
            axes = early if i == FAR_FIRST else late
            spots = [sum(((r >> axes[::-1].index(axis)) & 1) << d for d, axis in enumerate(late[::-1])) for r in range(parts)]
            size_of = block
        else:
            spots, size_of = list(range(half // 128)), 128
        keep, leave = run(
            functools.partial(grad_kernel, spots, size_of),
            "grad",
            (shape, shape),
            (mine, theirs, dpres[i], dpres_other[i]),
        )
        if paired:
            sums.append(Reduction(order, parts, axes, keep, leave))
            return
        both = jnp.concatenate([keep, leave]).astype(F32)
        sums.append(lax.psum_scatter(both, "parts", scatter_dimension=0, tiled=True))

    extra = max(128, width // parts)
    pieces = (far if DIRECT else 2) if paired else 1
    for step, cost in zip(PLAN, COSTS):
        kind, number = step[0], int(step[1:] or 0)
        order.cost = cost
        if kind == "g":
            gelu(number)
        elif kind == "f":
            mine, theirs = run(
                functools.partial(finish_kernel, late, block),
                "finish_mixed",
                (sds((half, rows), BF16), sds((half, rows), BF16)),
                (recv_row, ratio_row, mixed_t, *arrived),
                scalars=(place,),
            )
            theirs = lax.ppermute(theirs, "mp", SWAP)
        elif kind == "d":
            grad(number, mine, theirs)
        elif kind == "s":
            sent = run(
                functools.partial(
                    sent_kernel, len(CHUNKS), parts, per_part, first if paired else [list(range(parts))]
                ),
                "sent_grads",
                (sds((slots // pieces, width + extra), BF16),) * pieces,
                (back_row, ratio_row, *dpres, *bias_terms),
                scalars=(place,),
                scratch=[pltpu.VMEM((8, width), F32)],
            )
            if paired:
                swap = move(sent, near) if DIRECT else Exchange(order, parts, back, per_part, sent)
            else:
                returned = [exchange(sent[0])]
        elif kind == "b":
            (dtotal,) = run(
                functools.partial(back_kernel, len(CHUNKS)),
                "back",
                (sds((rows, half), BF16),),
                (ratio, (weight, other)[number], *dpres),
            )
            dtotals.append(dtotal)
        elif kind == "l":
            (partial,) = run(local_kernel, "input_local", (sds((rows, half), F32),), (adj_t, dtotals[number]))
            partials.append(partial)
        elif kind == "i":
            if paired:
                returned = swap if DIRECT else [swap.stay, swap.arrived]
            (bias_mine,) = run(bias_kernel, "bias_sum", (sds((1, extra), F32),), returned)
            bias_theirs = lax.ppermute(bias_mine, "mp", SWAP)
            size = min(512, half)
            (input_grad,) = run(
                input_kernel,
                "input_gradient",
                (sds((rows, width), BF16),),
                (send_row, *partials, weight, other, *returned),
                scalars=(place,),
                scratch=[pltpu.VMEM((width // size, rows, size), BF16), pltpu.SemaphoreType.DMA((width // size,))],
                keep=None,
            )
        elif paired and kind == "r":
            if JOIN and number == 1 and len(sums[1].axes) == digits - 2:
                sums[1].join(sums[0])
            sums[number].step()
        elif paired and kind == "e":
            if DIRECT:
                swap = move(
                    run(
                        functools.partial(regroup_kernel, per_part, [[(k, j) for k in range(far)] for j in range(near)]),
                        "regroup",
                        (sds((far * per_part, width + extra), BF16),) * near,
                        swap,
                    ),
                    1,
                )
            else:
                swap.step()
    count = width // (2 * parts)
    if paired:
        weight_grad, bias_grad = run(
            last_kernel,
            "last_sum",
            (sds((block, width), F32), sds((1, count), F32)),
            [bias_mine, bias_theirs] + sum((s.flat() for s in sums), []),
            scalars=(place,),
        )
        bias_grad = bias_grad.reshape(count)
    else:
        weight_grad = jnp.concatenate(sums, axis=1)
        bias_all = (bias_mine + bias_theirs)[0]
        bias_grad = jnp.where(core == 0, bias_all[:count], bias_all[count : 2 * count])
    return (
        act.reshape(batches, nodes, width),
        input_grad.reshape(batches, nodes, width),
        weight_grad,
        bias_grad,
    )


def solution(mesh):
    return jax.shard_map(
        functools.partial(local, mesh.shape["parts"]),
        mesh=mesh,
        in_specs=(
            P("mp", "parts", None),
            P("mp", None),
            P("mp"),
            P("mp", "parts", None),
            P("mp", "parts", None, None),
            P("mp", "parts", None, None),
            P("mp", "parts", None),
        ),
        out_specs=(
            P("mp", "parts", None),
            P("mp", "parts", None),
            P(("parts", "mp"), None),
            P(("parts", "mp")),
        ),
        check_vma=False,
    )
```
